32 devices in a mesh: dp: 4 (over y, x), seq: 8 (over z, core).
Axes of the slice: x: 2, y: 2, z: 4, core: 2. Of those that a mesh axis runs over, the one named last changes fastest.
Arguments:
- inputs: bfloat16 [4, 4096, 1024], P('dp', 'seq'), may hold values from -6 to 6
- out_grad: bfloat16 [4, 4096, 1024], P('dp', 'seq'), may hold values from -6 to 6
- w_in: bfloat16 [1024, 3072], replicated, may hold values from -0.1875 to 0.1875
- taps: float32 [3, 3072], replicated, may hold values from -3 to 3
- filt: bfloat16 [16, 256, 1024], P(None, 'seq'), may hold values from -4 to 4
Outputs:
- mixed: bfloat16 [4, 4096, 1024], P('dp', 'seq')
- in_grad: bfloat16 [4, 4096, 1024], P('dp', 'seq')
- w_in_grad: float32 [1024, 3072], P('dp', 'seq')
- taps_grad: float32 [3, 3072], replicated
The draws below stay inside these ranges and needn't reach their ends.
All inputs are finite; a program needn't handle non-finite values.
Results may differ from the reference program's by a relative error of at most 0.012.
Values may be sent and summed in bfloat16 or wider, within the bound.
No kernel may reach another device: no remote copies, remote signals or barrier semaphores. Data moves between devices by JAX's collectives and lax.ppermute only.
A program may use at most 128 MiB of HBM per device.

```python
import math
import jax
import jax.numpy as jnp
from jax import lax

D = 1024
BLK = 256
LENGTH = 4096
SEQS = 4
SPAN = 16


def draw_taps(key, part):
    normal = jax.random.normal(key, (3, 3 * D), jnp.float32)
    spread = jnp.array([1.0, 0.3, 1.0], jnp.float32)[:, None]
    return jnp.clip(normal * spread, -3.0, 3.0)


def block_levels(rng, shape, split, smallest, high):
    def one(dim, blocks):
        draws = jax.random.uniform(jax.random.fold_in(jax.random.fold_in(rng, 6), dim), (blocks,), jnp.float32, smallest / len(split), high / len(split))
        return jnp.repeat(jnp.exp(draws), shape[dim] // blocks).reshape((-1,) + (1,) * (len(shape) - dim - 1))

    factor_of = one(*split[0])
    for cut in split[1:]:
        factor_of = factor_of * one(*cut)
    return factor_of


def scatter_about(own_key, dims, deviation, most, shards=(), held_as=jnp.bfloat16):
    values = deviation * jax.random.normal(own_key, dims, jnp.float32)
    if shards:
        values = values * block_levels(own_key, dims, shards, -0.22, 0.18)
    return jnp.clip(values, -most, most).astype(held_as)


def setup_inputs(seed: int = 0) -> dict:
    key_of = jax.random.split(jax.random.key(seed), 6)
    inputs = scatter_about(key_of[0], (SEQS, LENGTH, D), 1.0, 6.0, ((0, 4), (1, 8)))
    out_grad = scatter_about(key_of[1], (SEQS, LENGTH, D), 1.0, 6.0, ((0, 4), (1, 8)))
    w_in = scatter_about(key_of[2], (D, 3 * D), D ** -0.5, 0.1875)
    taps = draw_taps(jax.random.fold_in(key_of[5], 71), 0)
    filt = scatter_about(key_of[4], (SPAN, BLK, D), 1.0, 4.0, ((1, 8),))
    return dict(inputs=inputs, out_grad=out_grad, w_in=w_in, taps=taps, filt=filt)


def dct_table(count):
    rows = jnp.arange(count, dtype=jnp.float32)[:, None]
    cols = jnp.arange(count, dtype=jnp.float32)[None, :]
    first = jnp.where(rows == 0, jnp.float32(math.sqrt(0.5)), jnp.float32(1.0))
    table = jnp.float32(math.sqrt(2.0 / count)) * first * jnp.cos(jnp.float32(math.pi) * (cols + 0.5) * rows / count)
    return table.astype(jnp.bfloat16)

def monarch(source, filt, table_q, table_p):
    hi = lax.Precision.HIGHEST
    blocks = source.reshape(SPAN, BLK, D).astype(jnp.float32)
    tq = table_q.astype(jnp.float32)
    tp = table_p.astype(jnp.float32)
    first = jnp.einsum('rq,pqd->prd', tq, blocks, precision=hi).astype(jnp.bfloat16)
    second = jnp.einsum('ap,prd->ard', tp, first.astype(jnp.float32), precision=hi)
    scaled = (filt.astype(jnp.float32) * second).astype(jnp.bfloat16)
    third = jnp.einsum('ap,ard->prd', tp, scaled.astype(jnp.float32), precision=hi).astype(jnp.bfloat16)
    last = jnp.einsum('rq,prd->pqd', tq, third.astype(jnp.float32), precision=hi)
    return last.reshape(LENGTH, D)

def reference(inputs, out_grad, w_in, taps, filt):
    table_q = dct_table(BLK)
    table_p = dct_table(SPAN)
    factor = 1.0 / math.sqrt(SEQS * LENGTH)

    def one(carry, pair):
        rows, grads = pair
        z = jnp.dot(rows, w_in, preferred_element_type=jnp.float32).astype(jnp.bfloat16)
        zpad = jnp.pad(z, ((1, 1), (0, 0)))
        s = taps[0] * zpad[:-2] + taps[1] * zpad[1:-1] + taps[2] * zpad[2:]
        a_part = s[:, :D]
        g_part = s[:, D:2 * D]
        v_part = s[:, 2 * D:]
        w = (a_part * v_part).astype(jnp.bfloat16)
        gradf = grads.astype(jnp.float32)
        e4 = (gradf * g_part).astype(jnp.bfloat16)
        h4 = monarch(w, filt, table_q, table_p)
        dw = monarch(e4, filt, table_q, table_p)
        mixed = (g_part * h4).astype(jnp.bfloat16)
        ds = jnp.concatenate([dw * v_part, gradf * h4, dw * a_part], axis=1).astype(jnp.bfloat16)
        dspad = jnp.pad(ds, ((1, 1), (0, 0)))
        du = (taps[0] * dspad[2:] + taps[1] * dspad[1:-1] + taps[2] * dspad[:-2]).astype(jnp.bfloat16)
        in_grad = jnp.dot(du, w_in.T, preferred_element_type=jnp.float32).astype(jnp.bfloat16)
        wgrad = jnp.dot(rows.T, du, preferred_element_type=jnp.float32)
        dsf = ds.astype(jnp.float32)
        zf = zpad.astype(jnp.float32)
        tgrad = jnp.stack([lax.optimization_barrier(jnp.sum(dsf * zf[k:k + LENGTH], axis=0)) for k in range(3)])
        return ((carry[0] + wgrad, carry[1] + tgrad), (mixed, in_grad))
    init = (jnp.zeros((D, 3 * D), jnp.float32), jnp.zeros((3, 3 * D), jnp.float32))
    (wgrad, tgrad), (mixed, in_grad) = lax.scan(one, init, (inputs, out_grad))
    return (mixed, in_grad, wgrad * factor, tgrad * factor)
```

```python
import functools
import math

import jax
import jax.numpy as jnp
from jax import lax
from jax.experimental import pallas as pl
from jax.experimental.pallas import tpu as pltpu
from jax.sharding import Mesh
from jax.sharding import PartitionSpec as P

BLK = 256
BF = jnp.bfloat16
F32 = jnp.float32
PARAMS = dict(vmem_limit_bytes=48 * 1024 * 1024)


def dct_table(count):
    rows = jnp.arange(count, dtype=jnp.float32)[:, None]
    cols = jnp.arange(count, dtype=jnp.float32)[None, :]
    first = jnp.where(rows == 0, jnp.float32(math.sqrt(0.5)), jnp.float32(1.0))
    table = (
        jnp.float32(math.sqrt(2.0 / count))
        * first
        * jnp.cos(jnp.float32(math.pi) * (cols + 0.5) * rows / count)
    )
    return table.astype(jnp.bfloat16)


def dot(left, right):
    return jnp.dot(left, right, preferred_element_type=F32)


def dot_nt(left, right):
    return lax.dot_general(left, right, (((1,), (1,)), ((), ())), preferred_element_type=F32)


def neighbours(cells, before, after):
    count = cells.shape[0]
    row = lax.broadcasted_iota(jnp.int32, cells.shape, 0)
    earlier = jnp.where(row == 0, before, pltpu.roll(cells, 1, 0))
    later = jnp.where(row == count - 1, after, pltpu.roll(cells, count - 1, 0))
    return earlier, later


def short_conv(cells, edge, taps):
    earlier, later = neighbours(cells, edge[0:1], edge[1:2])
    return taps[0:1] * earlier + taps[1:2] * cells + taps[2:3] * later


def put_blocks(table, cells, out_ref):
    owners, blocks, each = out_ref.shape[0], out_ref.shape[1], out_ref.shape[2]
    for p in range(blocks):
        h = dot(table, cells[p * BLK : (p + 1) * BLK])
        if each % 16 == 0:
            h = h.astype(BF)
        for k in range(owners):
            out_ref[k, p] = h[k * each : (k + 1) * each].astype(BF)


def take_block(ref, p):
    owners, each, width = ref.shape[0], ref.shape[2], ref.shape[3]
    h = ref[:, p]
    if each % 16:
        return h.astype(F32).reshape(owners * each, width).astype(BF)
    return h.reshape(owners * each, width)


def grad_block_kernel(x_ref, xh_ref, w_ref, taps_ref, og_ref, tq_ref, h_ref, z_ref, zh_ref):
    z = dot(x_ref[...], w_ref[...]).astype(BF)
    zh = dot(xh_ref[...], w_ref[...]).astype(BF)
    z_ref[...] = z
    zh_ref[...] = zh
    g = short_conv(z.astype(F32), zh.astype(F32), taps_ref[...])
    e4 = (og_ref[...].astype(F32) * g).astype(BF)
    put_blocks(tq_ref[...], e4, h_ref)


def value_block_kernel(
    x_ref, xh_ref, wa_ref, wv_ref, ta_ref, tv_ref, tq_ref, h_ref, za_ref, zv_ref, zha_ref, zhv_ref
):
    parts = []
    for w_ref, t_ref, z_ref, zh_ref in (
        (wa_ref, ta_ref, za_ref, zha_ref),
        (wv_ref, tv_ref, zv_ref, zhv_ref),
    ):
        z = dot(x_ref[...], w_ref[...]).astype(BF)
        zh = dot(xh_ref[...], w_ref[...]).astype(BF)
        z_ref[...] = z
        zh_ref[...] = zh
        parts.append(short_conv(z.astype(F32), zh.astype(F32), t_ref[...]))
    put_blocks(tq_ref[...], (parts[0] * parts[1]).astype(BF), h_ref)


def span_kernel(h_ref, filt_ref, k_ref, kt_ref, out_ref):
    span, group, width = h_ref.shape
    h, filt = h_ref[...], filt_ref[...]
    if group % 16:
        h = h.astype(F32)
    second = dot(k_ref[...], h.reshape(span * group, width).astype(BF))
    scaled = (filt.astype(F32).reshape(span * group, width) * second).astype(BF)
    third = dot(kt_ref[...], scaled)
    if group % 16 == 0:
        third = third.astype(BF)
    out_ref[...] = third.reshape(span, group, width).astype(BF)


def tap_sums(ds, z, zh, out_ref):
    dsf = ds.astype(F32)
    zf = z.astype(F32)
    zhf = zh.astype(F32)
    earlier, later = neighbours(zf, zhf[0:1], zhf[1:2])
    out_ref[0:1] = jnp.sum(dsf * earlier, axis=0, keepdims=True)
    out_ref[1:2] = jnp.sum(dsf * zf, axis=0, keepdims=True)
    out_ref[2:3] = jnp.sum(dsf * later, axis=0, keepdims=True)


def inverse(h_ref, tqt_ref):
    blocks = h_ref.shape[1]
    return jnp.concatenate([dot(tqt_ref[...], take_block(h_ref, p)) for p in range(blocks)], axis=0)


def emit(ds, z_ref, zh_ref, ds_ref, edge_ref, sums_ref):
    tok = ds.shape[0]
    ds_ref[...] = ds
    dsf = ds.astype(F32)
    edge_ref[...] = jnp.concatenate([dsf[0:1], dsf[tok - 1 : tok]], axis=0).astype(BF)
    tap_sums(ds, z_ref[...], zh_ref[...], sums_ref)


def grad_out_kernel(
    h_ref, tqt_ref, za_ref, zv_ref, zha_ref, zhv_ref, ta_ref, tv_ref,
    dsa_ref, dsv_ref, ea_ref, ev_ref, sa_ref, sv_ref,
):
    dw = inverse(h_ref, tqt_ref)
    v = short_conv(zv_ref[...].astype(F32), zhv_ref[...].astype(F32), tv_ref[...])
    emit((dw * v).astype(BF), za_ref, zha_ref, dsa_ref, ea_ref, sa_ref)
    a = short_conv(za_ref[...].astype(F32), zha_ref[...].astype(F32), ta_ref[...])
    emit((dw * a).astype(BF), zv_ref, zhv_ref, dsv_ref, ev_ref, sv_ref)


def value_out_kernel(
    h_ref, tqt_ref, zg_ref, zhg_ref, tg_ref, og_ref, mixed_ref, dsg_ref, eg_ref, sg_ref
):
    h4 = inverse(h_ref, tqt_ref)
    g = short_conv(zg_ref[...].astype(F32), zhg_ref[...].astype(F32), tg_ref[...])
    mixed_ref[...] = (g * h4).astype(BF)
    emit((og_ref[...].astype(F32) * h4).astype(BF), zg_ref, zhg_ref, dsg_ref, eg_ref, sg_ref)


def du_of(ds_ref, dh_ref, taps_ref):
    ds = ds_ref[...].astype(F32)
    dh = dh_ref[...].astype(F32)
    taps = taps_ref[...]
    earlier, later = neighbours(ds, dh[0:1], dh[1:2])
    return (taps[0:1] * later + taps[1:2] * ds + taps[2:3] * earlier).astype(BF)


def du_first_kernel(
    dsa_ref, dsv_ref, dha_ref, dhv_ref, ta_ref, tv_ref, wa_ref, wv_ref, dua_ref, duv_ref, acc_ref
):
    dua = du_of(dsa_ref, dha_ref, ta_ref)
    duv = du_of(dsv_ref, dhv_ref, tv_ref)
    dua_ref[...] = dua
    duv_ref[...] = duv
    part = dot_nt(dua, wa_ref[...]) + dot_nt(duv, wv_ref[...])

    @pl.when(pl.program_id(0) == 0)
    def _():
        acc_ref[...] = part

    @pl.when(pl.program_id(0) > 0)
    def _():
        acc_ref[...] += part


def du_last_kernel(dsg_ref, dhg_ref, tg_ref, wg_ref, first_ref, dug_ref, out_ref, acc_ref):
    dug = du_of(dsg_ref, dhg_ref, tg_ref)
    dug_ref[...] = dug
    part = dot_nt(dug, wg_ref[...])

    @pl.when(pl.program_id(0) == 0)
    def _():
        acc_ref[...] = first_ref[...] + part

    @pl.when(pl.program_id(0) > 0)
    def _():
        acc_ref[...] += part

    @pl.when(pl.program_id(0) == pl.num_programs(0) - 1)
    def _():
        out_ref[...] = acc_ref[...].astype(BF)


def w_grad_kernel(xo_ref, xp_ref, do_ref, dp_ref, out_ref):
    part = dot(xo_ref[...], do_ref[...]) + dot(xp_ref[...], dp_ref[...])
    out_ref[...] = part.astype(BF).reshape(out_ref.shape)


def shards(inputs, out_grad, w_in, taps, filt):
    tok, width = inputs.shape[1], inputs.shape[2]
    ndp, nz, ncore = lax.axis_size("dp"), lax.axis_size("z"), lax.axis_size("core")
    nseq = nz * ncore
    span, each = filt.shape[0], filt.shape[1]
    nblocks = tok // BLK
    seq = ("z", "core")
    core = lax.axis_index("core")
    factor = 1.0 / math.sqrt(ndp * nseq * tok)
    cb = 256
    ncb = width // cb
    tq = dct_table(BLK)
    tp = dct_table(span)
    group = math.gcd(each, 16)
    kron = jnp.kron(tp, jnp.eye(group, dtype=BF))
    x = inputs[0]
    og = out_grad[0]

    fwd = [(i, i + 1) for i in range(nseq - 1)]
    bwd = [(i + 1, i) for i in range(nseq - 1)]

    def halo(first, last):
        return lax.ppermute(last, seq, fwd), lax.ppermute(first, seq, bwd)

    before, after = halo(x[0:1], x[tok - 1 : tok])
    xh = jnp.concatenate([before, after, jnp.zeros((14, width), BF)], axis=0)

    def S(shape, dtype=BF):
        return jax.ShapeDtypeStruct(shape, dtype)

    full = lambda *shape: pl.BlockSpec(shape, lambda j: (0,) * len(shape))
    col = lambda rows, off=0: pl.BlockSpec((rows, cb), lambda j: (0, off * ncb + j))
    chunk = pl.BlockSpec((nseq, nblocks, each, cb), lambda j: (0, 0, 0, j))
    hshape = S((nseq, nblocks, each, width))

    def call(kernel, name, ins, in_specs, outs, out_specs, flops, scratch=(), grid=None):
        moved = sum(a.size * a.dtype.itemsize for a in (*ins, *outs))
        return pl.pallas_call(
            kernel,
            out_shape=outs,
            grid=grid or (ncb,),
            in_specs=in_specs,
            out_specs=out_specs,
            scratch_shapes=scratch,
            compiler_params=pltpu.CompilerParams(**PARAMS),
            cost_estimate=pl.CostEstimate(flops=flops, bytes_accessed=moved, transcendentals=0),
            name=name,
        )(*ins)

    mm = 2 * tok * width * width
    he, zg, zhg = call(
        grad_block_kernel, "grad_block",
        (x, xh, w_in, taps, og, tq),
        [full(tok, width), full(16, width), col(width, 1), col(3, 1), col(tok), full(BLK, BLK)],
        (hshape, S((tok, width)), S((16, width))),
        (chunk, col(tok), col(16)),
        mm + mm // 4,
    )
    hw, za, zv, zha, zhv = call(
        value_block_kernel, "value_block",
        (x, xh, w_in, w_in, taps, taps, tq),
        [full(tok, width), full(16, width), col(width, 0), col(width, 2), col(3, 0), col(3, 2), full(BLK, BLK)],
        (hshape, S((tok, width)), S((tok, width)), S((16, width)), S((16, width))),
        (chunk, col(tok), col(tok), col(16), col(16)),
        2 * mm + mm // 4,
    )

    def swap(h):
        return lax.all_to_all(h, seq, 0, 0, tiled=True)

    def span_step(h):
        wide = 512
        block = pl.BlockSpec((span, group, wide), lambda i, j: (0, i, j))
        table = pl.BlockSpec(kron.shape, lambda i, j: (0, 0))
        out = call(
            span_kernel, "span",
            (h.reshape(span, each, width), filt, kron, kron.T),
            [block, block, table, table],
            (S((span, each, width)),),
            (block,),
            mm // 2,
            grid=(each // group, width // wide),
        )
        return out[0].reshape(h.shape)

    ce = swap(he)
    cw = swap(hw)
    be = swap(span_step(ce))
    bw = swap(span_step(cw))

    tqt = tq.T
    dsa, dsv, ea, ev, sa, sv = call(
        grad_out_kernel, "grad_out",
        (be, tqt, za, zv, zha, zhv, taps, taps),
        [chunk, full(BLK, BLK), col(tok), col(tok), col(16), col(16), col(3, 0), col(3, 2)],
        (S((tok, width)), S((tok, width)), S((2, width)), S((2, width)), S((3, width), F32), S((3, width), F32)),
        (col(tok), col(tok), col(2), col(2), col(3), col(3)),
        mm // 4,
    )

    def edges(*parts):
        both = jnp.concatenate(parts, axis=1)
        before, after = halo(both[0:1], both[1:2])
        return jnp.concatenate([before, after], axis=0)

    dh = edges(ea, ev)
    dua, duv, acc = call(
        du_first_kernel, "du_first",
        (dsa, dsv, dh, dh, taps, taps, w_in, w_in),
        [col(tok), col(tok), col(2, 0), col(2, 1), col(3, 0), col(3, 2), col(width, 0), col(width, 2)],
        (S((tok, width)), S((tok, width)), S((tok, width), F32)),
        (col(tok), col(tok), full(tok, width)),
        2 * mm,
    )

    half = width // ndp // ncore
    xt = x.T.reshape(ndp, ncore, half, tok)
    pick = lambda c: lax.dynamic_index_in_dim(xt, c, 1, keepdims=False).reshape(ndp * half, tok)
    flip = [(0, 1), (1, 0)]
    xo = pick(core)
    xp = lax.ppermute(pick(1 - core), "core", flip)
    rows = ndp * half

    def w_grad(du):
        other = lax.ppermute(du, "core", flip)
        part = call(
            w_grad_kernel, "w_grad",
            (xo, xp, du, other),
            [full(rows, tok), full(rows, tok), col(tok), col(tok)],
            (S((ndp, half, width)),),
            (pl.BlockSpec((ndp, half, cb), lambda j: (0, 0, j)),),
            mm,
        )[0]
        got = lax.all_to_all(part, "dp", 0, 0, tiled=True)
        return jnp.sum(got.astype(F32), axis=0).astype(BF)

    def all_sum(value):
        for axis, count in (("core", ncore), ("z", nz), ("dp", ndp)):
            step = 1
            while step < count:
                value = value + lax.ppermute(value, axis, [(i, i ^ step) for i in range(count)])
                step *= 2
        return value

    wa, wv = w_grad(dua), w_grad(duv)
    t_av = all_sum(jnp.concatenate([sa, sv], axis=0))

    mixed, dsg, eg, sg = call(
        value_out_kernel, "value_out",
        (bw, tqt, zg, zhg, taps, og),
        [chunk, full(BLK, BLK), col(tok), col(16), col(3, 1), col(tok)],
        (S((tok, width)), S((tok, width)), S((2, width)), S((3, width), F32)),
        (col(tok), col(tok), col(2), col(3)),
        mm // 4,
    )
    dhg = edges(eg)
    dug, in_grad = call(
        du_last_kernel, "du_last",
        (dsg, dhg, taps, w_in, acc),
        [col(tok), col(2), col(3, 1), col(width, 1), full(tok, width)],
        (S((tok, width)), S((tok, width))),
        (col(tok), full(tok, width)),
        mm,
        scratch=[pltpu.VMEM((tok, width), F32)],
    )
    wg = w_grad(dug)
    t_g = all_sum(sg)
    taps_grad = jnp.concatenate([t_av[0:3], t_g, t_av[3:6]], axis=1) * factor

    own = 3 * width // nseq
    wide = jnp.concatenate([wa, wg, wv], axis=1).reshape(half, nseq, own).transpose(1, 0, 2)
    got = lax.all_to_all(wide, seq, 0, 0, tiled=True).reshape(nz, ncore * half, own)
    w_in_grad = jnp.sum(got.astype(F32), axis=0) * factor
    return (mixed[None], in_grad[None], w_in_grad, taps_grad)


def solution(mesh):
    ndp, nseq = mesh.shape["dp"], mesh.shape["seq"]
    split = Mesh(mesh.devices.reshape(ndp, nseq // 2, 2), ("dp", "z", "core"))
    seq = ("z", "core")
    return jax.shard_map(
        shards,
        mesh=split,
        in_specs=(P("dp", seq, None), P("dp", seq, None), P(), P(), P(None, seq, None)),
        out_specs=(P("dp", seq, None), P("dp", seq, None), P("dp", seq), P()),
        check_vma=False,
    )
```

```python
import functools
import math

import jax
import jax.numpy as jnp
import numpy as np
from jax import lax
from jax.experimental import pallas as pl
from jax.experimental.pallas import tpu as pltpu
from jax.sharding import Mesh
from jax.sharding import PartitionSpec as P

BLK = 256
BF = jnp.bfloat16
EDGE = 16
NW = 2
SHADE = 1000
AV_DONE = 3
E_WHOLE, W_WHOLE, AV_WHOLE, G_WHOLE = False, False, False, False
F32 = jnp.float32
PARAMS = dict(vmem_limit_bytes=48 * 1024 * 1024)


def dct_table(count):
    one = np.float32
    rows = np.arange(count, dtype=np.float32)[:, None]
    cols = np.arange(count, dtype=np.float32)[None, :]
    first = np.where(rows == 0, one(math.sqrt(0.5)), one(1.0))
    table = one(math.sqrt(2.0 / count)) * first * np.cos(one(math.pi) * (cols + one(0.5)) * rows / one(count))
    return table.astype(BF)


def dot(left, right):
    return jnp.dot(left, right, preferred_element_type=F32)


def dot_nt(left, right):
    return lax.dot_general(left, right, (((1,), (1,)), ((), ())), preferred_element_type=F32)


def neighbours(cells, before, after):
    count = cells.shape[0]
    row = lax.broadcasted_iota(jnp.int32, cells.shape, 0)
    earlier = jnp.where(row == 0, before, pltpu.roll(cells, 1, 0))
    later = jnp.where(row == count - 1, after, pltpu.roll(cells, count - 1, 0))
    return earlier, later


def short_conv(cells, edge, taps):
    earlier, later = neighbours(cells, edge[0:1], edge[1:2])
    return taps[0:1] * earlier + taps[1:2] * cells + taps[2:3] * later


def lanes(width):
    step = min(width, 256)
    return [(at, pl.ds(at, step)) for at in range(0, width, step)]


def mine(off, width, at, step):
    start = lax.axis_index("core") * width + (off + at)
    return pl.ds(pl.multiple_of(start, 128), step)


def part_of(core, size):
    if isinstance(core, int):
        return pl.ds(core * size, size)
    return pl.ds(pl.multiple_of(core * size, size), size)


def ordered(first, second):
    swap = lax.axis_index("core") == 1
    return jnp.where(swap, second, first), jnp.where(swap, first, second)


def pieces(refs, axis):
    size = lax.axis_size(axis)
    if len(refs) == 1:
        return [(k, refs[0].at[k]) for k in range(size)]
    return [(lax.axis_index(axis) ^ k, ref) for k, ref in enumerate(refs)]


def pack_kernel(x_ref, og_ref, ends_ref, send_ref):
    core, tok, width = lax.axis_index("core"), x_ref.shape[0], send_ref.shape[1]
    x_head, x_tail = x_ref[0:16, :].astype(F32)[0:2], x_ref[tok - 16 : tok, :].astype(F32)[14:16]
    g_head, g_tail = og_ref[0:16, :].astype(F32)[0:1], og_ref[tok - 16 : tok, :].astype(F32)[15:16]
    first = core == 0
    rows = [jnp.where(first, x_head, x_tail), jnp.where(first, g_head, g_tail)]
    rows.append(jnp.zeros((EDGE - 3, x_ref.shape[1]), F32))
    ends_ref[...] = jnp.concatenate(rows, axis=0).astype(BF)
    send_ref[...] = og_ref[:, part_of(1 - core, width)]


def edge_rows(first_ref, second_ref):
    before, after = ordered(first_ref[...].astype(F32), second_ref[...].astype(F32))
    pad = jnp.zeros((EDGE - 4, before.shape[1]), F32)
    return jnp.concatenate([before[1:2], after[0:1], before[0:1], after[1:2], pad], axis=0).astype(BF)


def project(x_ref, xs_ref, xh, w, z_ref, zh_ref, here):
    core, tok = lax.axis_index("core"), x_ref.shape[0]
    z_ref[part_of(core, tok), here] = dot(x_ref[...], w).astype(BF)
    z_ref[part_of(1 - core, tok), here] = dot(xs_ref[...], w).astype(BF)
    zh = dot(xh, w).astype(BF)
    zh_ref[:, here] = zh
    return z_ref[:, here].astype(F32), zh.astype(F32)


def put_blocks(table, cells, hold, here):
    for p in range(hold.shape[0]):
        hold[p, :, here] = dot(table, cells[p * BLK : (p + 1) * BLK]).astype(BF)


def hand_rows(hold, outs, cols):
    for there, out in pieces(outs, "z"):
        out[...] = hold[:, part_of(there, out.shape[1]), cols]


def grad_block_kernel(
    n, x_ref, xs_ref, h1_ref, h2_ref, w_ref, taps_ref, og_ref, ogs_ref, tq_ref, *refs
):
    outs, (z_ref, zh_ref, og_all_ref, hold) = refs[:n], refs[n:]
    core, tok = lax.axis_index("core"), x_ref.shape[0]
    width = z_ref.shape[1]
    og_all_ref[part_of(core, tok), :] = og_ref[:, part_of(core, width)]
    og_all_ref[part_of(1 - core, tok), :] = ogs_ref[...]
    xh = edge_rows(h1_ref, h2_ref)
    for at, here in lanes(width):
        cols = mine(2 * width, width, at, here.size)
        z, zh = project(x_ref, xs_ref, xh, w_ref[:, cols], z_ref, zh_ref, here)
        g = short_conv(z, zh, taps_ref[:, cols])
        e4 = (og_all_ref[:, here].astype(F32) * g).astype(BF)
        put_blocks(tq_ref[...], e4, hold, here)
    hand_rows(hold, outs, pl.ds(0, width))


def value_block_kernel(
    n, nw, x_ref, xs_ref, h1_ref, h2_ref, w_ref, taps_ref, tq_ref, after_ref, *refs
):
    outs, (za_ref, zv_ref, zha_ref, zhv_ref, xt_ref, hold) = refs[: n * nw], refs[n * nw :]
    core, tok = lax.axis_index("core"), x_ref.shape[0]
    width = za_ref.shape[1]
    xh = edge_rows(h1_ref, h2_ref)
    for at, here in lanes(width):
        parts = []
        for off, z_ref, zh_ref in ((0, za_ref, zha_ref), (4 * width, zv_ref, zhv_ref)):
            cols = mine(off, width, at, here.size)
            z, zh = project(x_ref, xs_ref, xh, w_ref[:, cols], z_ref, zh_ref, here)
            parts.append(short_conv(z, zh, taps_ref[:, cols]))
        put_blocks(tq_ref[...], (parts[0] * parts[1]).astype(BF), hold, here)
    for i in range(nw):
        hand_rows(hold, outs[i * n : (i + 1) * n], pl.ds(i * (width // nw), width // nw))
    xt_ref[:, part_of(core, tok)] = x_ref[...].T
    xt_ref[:, part_of(1 - core, tok)] = xs_ref[...].T


def span_kernel(n, skip, off, *refs):
    ins, refs = refs[:n], refs[n + skip :]
    (filt_ref, filts_ref, k_ref, kt_ref, tq_ref), outs, (hold, filts) = refs[:5], refs[5 : n + 5], refs[n + 5 :]
    core, place, places = lax.axis_index("core"), lax.axis_index("z"), lax.axis_size("z")
    span, rows, width = hold.shape
    each, blocks = filt_ref.shape[1], span // places
    half = filts_ref.shape[2]
    group = k_ref.shape[0] // span
    for there, ref in pieces(ins, "z"):
        hold[pl.ds(there * blocks, blocks)] = ref[...]
    mine_at = pl.ds(pl.multiple_of(core * half + off, 128), width)
    filts[:, part_of(core, each), :] = filt_ref[:, :, mine_at].astype(filts.dtype)
    filts[:, part_of(1 - core, each), :] = filts_ref[:, :, off : off + width].astype(filts.dtype)
    for _, here in lanes(width):
        for at in range(0, rows, group):
            some = pl.ds(at, group)
            flat = (span * group, here.size)
            second = dot(k_ref[...], hold[:, some, here].reshape(flat))
            scaled = (filts[:, some, here].reshape(flat).astype(F32) * second).astype(BF)
            third = dot(kt_ref[...], scaled).astype(BF)
            hold[:, some, here] = third.reshape(span, group, here.size)
    table = tq_ref[part_of(place, rows), :].astype(F32)
    first_q, last_q = table[:, 0:1], table[:, BLK - 1 : BLK]
    for there, out in pieces(outs, "z"):
        for p in range(blocks):
            out[p * rows : (p + 1) * rows, :] = hold[there * blocks + p]
        sums = []
        for p, column, inside in (
            (there * blocks - 1, last_q, there > 0),
            (there * blocks + blocks, first_q, there < places - 1),
        ):
            cells = hold[jnp.clip(p, 0, span - 1)].astype(F32)
            total = jnp.sum(cells * column, axis=0, keepdims=True)
            sums.append(jnp.where(inside, total, 0.0))
        both = jnp.concatenate(sums, axis=0)
        high = both.astype(BF).astype(F32)
        pad = jnp.zeros((EDGE - 4, width), F32)
        out[blocks * rows :, :] = jnp.concatenate([high, both - high, pad], axis=0).astype(BF)


def take_rows(ins, hold):
    blocks = hold.shape[0]
    rows = hold.shape[1] // lax.axis_size("z")
    for there, ref in pieces(ins, "z"):
        for p in range(blocks):
            hold[p, part_of(there, rows), :] = ref[p * rows : (p + 1) * rows, :]


def inverse(ins, hold, tqt_ref, here):
    cells = jnp.concatenate([dot(tqt_ref[...], hold[p, :, here]) for p in range(hold.shape[0])], axis=0)
    shares = [ref for _, ref in pieces(ins, "z")]
    at = shares[0].shape[0] - EDGE
    edge = shares[0][at : at + EDGE, here].astype(F32)
    for ref in shares[1:]:
        edge = edge + ref[at : at + EDGE, here].astype(F32)
    return cells, edge[0:1] + edge[2:3], edge[1:2] + edge[3:4]


def conv_wide(z, zh, taps):
    count = z.shape[0]
    before = taps[0:1] * zh[2:3] + taps[1:2] * zh[0:1] + taps[2:3] * z[0:1]
    after = taps[0:1] * z[count - 1 : count] + taps[1:2] * zh[1:2] + taps[2:3] * zh[3:4]
    return short_conv(z, zh, taps), before, after


def rounded(value):
    return value.astype(BF).astype(F32)


def emit(cells, gate, z, zh, taps, cols, du_ref, sums_ref):
    ds, before, after = (rounded(one * two) for one, two in zip(cells, gate))
    earlier, later = neighbours(ds, before, after)
    du_ref[:, cols] = (taps[0:1] * later + taps[1:2] * ds + taps[2:3] * earlier).astype(BF)
    earlier, later = neighbours(z, zh[0:1], zh[1:2])
    sums_ref[0:1, cols] = jnp.sum(ds * earlier, axis=0, keepdims=True)
    sums_ref[1:2, cols] = jnp.sum(ds * z, axis=0, keepdims=True)
    sums_ref[2:3, cols] = jnp.sum(ds * later, axis=0, keepdims=True)


def multiply(xt_ref, du_ref, outs, part):
    for _, here in lanes(du_ref.shape[1]):
        part[:, here] = dot(xt_ref[...], du_ref[:, here]).astype(BF)
    rows = part.shape[0] // lax.axis_size("dp")
    for there, out in pieces(outs, "dp"):
        out[0:rows, :] = part[part_of(there, rows), :]


def grad_out_kernel(n, nd, *refs):
    ins, refs = refs[:n], refs[n + 1 :]
    (tqt_ref, za_ref, zv_ref, zha_ref, zhv_ref, taps_ref, xt_ref), refs = refs[:7], refs[7:]
    (du_ref, send_ref, sums_ref), outs, (hold, part) = refs[:3], refs[3 : 3 + nd], refs[3 + nd :]
    width, tok = za_ref.shape[1], send_ref.shape[0]
    take_rows(ins, hold)
    for at, here in lanes(width):
        dw = inverse(ins, hold, tqt_ref, here)
        za, zha = za_ref[:, here].astype(F32), zha_ref[:, here].astype(F32)
        zv, zhv = zv_ref[:, here].astype(F32), zhv_ref[:, here].astype(F32)
        ta = taps_ref[:, mine(0, width, at, here.size)]
        tv = taps_ref[:, mine(4 * width, width, at, here.size)]
        emit(dw, conv_wide(zv, zhv, tv), za, zha, ta, here, du_ref, sums_ref)
        emit(dw, conv_wide(za, zha, ta), zv, zhv, tv, pl.ds(width + at, here.size), du_ref, sums_ref)
    send_ref[...] = du_ref[part_of(1 - lax.axis_index("core"), tok), :]
    multiply(xt_ref, du_ref, outs, part)


def three_parts(value):
    high = rounded(value)
    middle = rounded(value - high)
    return [high, middle, value - high - middle]


def value_out_kernel(n, skip, off, *refs):
    ins, refs = refs[:n], refs[n + skip :]
    (tqt_ref, zg_ref, zhg_ref, taps_ref, og_ref, h1_ref, h2_ref), refs = refs[:7], refs[7:]
    (mo_ref, ms_ref, du_ref, send_ref, sums_ref), (hold, mixed) = refs[:5], refs[5:]
    core, tok, half = lax.axis_index("core"), mo_ref.shape[0], zg_ref.shape[1]
    width = mo_ref.shape[1]
    take_rows(ins, hold)
    for at, here in lanes(width):
        there = pl.ds(off + at, here.size)
        h4 = inverse(ins, hold, tqt_ref, here)
        z, zh = zg_ref[:, there].astype(F32), zhg_ref[:, there].astype(F32)
        cols = mine(2 * half, half, off + at, here.size)
        whole = mine(0, half, off + at, here.size)
        taps = taps_ref[:, cols]
        mixed[:, here] = (short_conv(z, zh, taps) * h4[0]).astype(BF)
        before, after = ordered(h1_ref[:, whole].astype(F32), h2_ref[:, whole].astype(F32))
        og = (og_ref[:, there].astype(F32), before[2:3], after[2:3])
        emit(h4, og, z, zh, taps, here, du_ref, sums_ref)
    mo_ref[...] = mixed[part_of(core, tok), :]
    ms_ref[...] = mixed[part_of(1 - core, tok), :]
    send_ref[...] = du_ref[part_of(1 - core, tok), :]


def w_grad_kernel(skip, known, *refs):
    refs = refs[skip:]
    (xt_ref, du_ref), known, outs, part = refs[:2], refs[2 : 2 + known], refs[2 + known : -1], refs[-1]
    multiply(xt_ref, du_ref, outs, part)
    if known:
        width = du_ref.shape[1]
        av = known[0][...]
        half = av.shape[1] // 2
        every = [av[:, :half], *(ref[...] for ref in known[1:]), av[:, half:]]
        every = jnp.concatenate(every, axis=1)
        lines = []
        for at in range(0, 3 * half, width):
            lines += three_parts(every[:, at : at + width])
        rows = part.shape[0] // lax.axis_size("dp")
        extra = outs[0].shape[-2] - rows
        lines.append(jnp.zeros((extra - 3 * len(lines), width), F32))
        block = jnp.concatenate(lines, axis=0).astype(BF)
        for _, out in pieces(outs, "dp"):
            out[rows : rows + extra, :] = block


def in_part(du_ref, rows, w_ref, columns, width):
    total = None
    for run, start in enumerate(columns):
        w = w_ref[:, pl.ds(pl.multiple_of(start, 128), width)]
        part = dot_nt(du_ref[rows, run * width : (run + 1) * width], w)
        total = part if total is None else total + part
    return total


def in_first_kernel(du_ref, got_ref, w_ref, after_ref, acc_ref):
    core, tok, width = lax.axis_index("core"), got_ref.shape[0], w_ref.shape[1] // 6
    every = pl.ds(0, tok)
    own = in_part(du_ref, part_of(core, tok), w_ref, [core * width, (4 + core) * width], width)
    acc_ref[...] = own + in_part(got_ref, every, w_ref, [(1 - core) * width, (5 - core) * width], width)


def in_last_kernel(nw, *refs):
    dus, gots, owns, others = (refs[i * nw : (i + 1) * nw] for i in range(4))
    w_ref, acc_ref, after_ref, out_ref, mixed_ref = refs[4 * nw :]
    core, half = lax.axis_index("core"), w_ref.shape[1] // 6
    tok, width = gots[0].shape
    total = acc_ref[...]
    for i in range(nw):
        for ref, rows, owner in (
            (dus[i], part_of(core, tok), core),
            (gots[i], pl.ds(0, tok), 1 - core),
        ):
            total = total + in_part(ref, rows, w_ref, [(2 + owner) * half + i * width], width)
        for ref, owner in ((owns[i], core), (others[i], 1 - core)):
            at = pl.multiple_of(owner * half + i * width, 128)
            mixed_ref[:, pl.ds(at, width)] = ref[...]
    out_ref[...] = total.astype(BF)


def add_all(values):
    while len(values) > 1:
        values = [one + two for one, two in zip(values[::2], values[1::2])]
    return values[0]


def fold_kernel(na, n, nw, *refs):
    av, refs = [ref for _, ref in pieces(refs[:na], "dp")], refs[na:]
    gs = [[ref for _, ref in pieces(refs[i * n : (i + 1) * n], "dp")] for i in range(nw)]
    own_ref, send_ref, taps_ref, hold = refs[n * nw :]
    core, width = lax.axis_index("core"), gs[0][0].shape[1]
    half_cols = width * nw
    rows = av[0].shape[0]
    both = add_all([ref[...].astype(F32) for ref in av]).astype(BF)
    hold[:, 0:half_cols] = both[:, :half_cols]
    for i, parts in enumerate(gs):
        at = half_cols + i * width
        hold[:, at : at + width] = add_all([ref[0:rows, :].astype(F32) for ref in parts]).astype(BF)
    hold[:, 2 * half_cols :] = both[:, half_cols:]
    half = own_ref.shape[0]
    own_ref[...] = hold[part_of(core, half), :]
    send_ref[...] = hold[part_of(1 - core, half), :]
    extra = gs[-1][0].shape[0] - rows
    sums = add_all([ref[rows : rows + extra, :].astype(F32) for ref in gs[-1]])
    for group in range(3 * nw):
        at = 9 * group
        value = sums[at : at + 3] + sums[at + 3 : at + 6] + sums[at + 6 : at + 9]
        taps_ref[:, group * width : (group + 1) * width] = value


def spread(own_ref, got_ref, out_ref):
    core, width = lax.axis_index("core"), own_ref.shape[1] // 3
    for run in range(3):
        cols = pl.ds(run * width, width)
        for ref, owner in ((own_ref, core), (got_ref, 1 - core)):
            at = pl.multiple_of((2 * run + owner) * width, 128)
            out_ref[:, pl.ds(at, width)] = ref[:, cols]


def join_kernel(own_ref, got_ref, after_ref, *refs):
    outs, hold = refs[:-1], refs[-1]
    spread(own_ref, got_ref, hold)
    for there, out in pieces(outs, "z"):
        out[...] = hold[:, part_of(there, out.shape[1])]


def sum_kernel(n, *refs):
    ins, (own_ref, send_ref) = refs[:n], refs[n:]
    core, width = lax.axis_index("core"), own_ref.shape[1]
    for out, owner in ((own_ref, core), (send_ref, 1 - core)):
        cols = part_of(owner, width)
        out[...] = add_all([ref[:, cols].astype(F32) for ref in ins])


def last_kernel(factor, own_ref, got_ref, t_own_ref, t_got_ref, out_ref, taps_ref):
    core, rows = lax.axis_index("core"), own_ref.shape[0]
    out_ref[part_of(core, rows), :] = own_ref[...] * factor
    out_ref[part_of(1 - core, rows), :] = got_ref[...] * factor
    spread(t_own_ref, t_got_ref, taps_ref)
    taps_ref[...] = taps_ref[...] * factor


def shards(nw, inputs, out_grad, w_in, taps, filt):
    tok, width = inputs.shape[1], inputs.shape[2]
    ndp, nz, ncore = lax.axis_size("dp"), lax.axis_size("z"), lax.axis_size("core")
    nseq = nz * ncore
    span, each = filt.shape[0], filt.shape[1]
    seq = ("z", "core")
    core = lax.axis_index("core")
    factor = 1.0 / math.sqrt(ndp * nseq * tok)
    wide, count = width // ncore, tok * ncore
    blocks, rows = count // BLK, each * ncore
    group = math.gcd(rows, 16)
    tq, tp = dct_table(BLK), dct_table(span)
    kron = np.kron(tp.astype(np.float32), np.eye(group, dtype=np.float32)).astype(BF)
    tq, tqt, kron, kront = (jnp.asarray(table) for table in (tq, tq.T.copy(), kron, kron.T.copy()))
    x, og = inputs[0], out_grad[0]

    def S(shape, dtype=BF):
        return jax.ShapeDtypeStruct(shape, dtype)

    def call(kernel, name, ins, outs, flops, scratch=(), shade=1):
        moved = sum(a.size * a.dtype.itemsize for a in (*ins, *outs))
        whole = pl.BlockSpec(memory_space=pltpu.VMEM)
        return pl.pallas_call(
            kernel,
            out_shape=outs,
            in_specs=[whole] * len(ins),
            out_specs=[whole] * len(outs),
            scratch_shapes=scratch,
            compiler_params=pltpu.CompilerParams(**PARAMS),
            cost_estimate=pl.CostEstimate(flops=flops // shade, bytes_accessed=moved // shade, transcendentals=0),
            name=name,
        )(*ins)

    def flip(value):
        return lax.ppermute(value, "core", [(0, 1), (1, 0)])

    def swap(parts, axis):
        size = lax.axis_size(axis)
        if len(parts) == 1:
            return [lax.all_to_all(parts[0], axis, 0, 0, tiled=True)]
        return [parts[0]] + [
            lax.ppermute(parts[k], axis, [(i, i ^ k) for i in range(size)]) for k in range(1, size)
        ]

    def parts_of(whole, axis, shape):
        size = lax.axis_size(axis)
        return [S((size, *shape))] if whole else [S(shape)] * size

    mm = 2 * tok * width * width
    xs = flip(x)
    ends, og_send = call(pack_kernel, "pack", (x, og), [S((EDGE, width)), S((tok, wide))], mm // 999)
    odd = range(1, nseq - 1, 2)
    near = [(i, i + 1) for i in odd] + [(i + 1, i) for i in odd]
    far = [(i, i + 2) for i in odd] + [(i + 1, i - 1) for i in odd]
    h1, h2 = lax.ppermute(ends, seq, near), lax.ppermute(ends, seq, far)
    ogs = flip(og_send)

    def hold_of(cols):
        return pltpu.VMEM((blocks, BLK, cols), BF)

    act, edge = S((count, wide)), S((EDGE, wide))
    e_parts = parts_of(E_WHOLE, "z", (blocks, rows, wide))
    *he, zg, zhg, og_all = call(
        functools.partial(grad_block_kernel, len(e_parts)), "grad_block",
        (x, xs, h1, h2, w_in, taps, og, ogs, tq), e_parts + [act, edge, act],
        mm + mm // 4, [hold_of(wide)],
    )
    ce = swap(he, "z")
    some = wide // nw
    w_parts = parts_of(W_WHOLE, "z", (blocks, rows, some))
    *hw, za, zv, zha, zhv, xt = call(
        functools.partial(value_block_kernel, len(w_parts), nw), "value_block",
        (x, xs, h1, h2, w_in, taps, tq, zhg),
        w_parts * nw + [act, act, edge, edge, S((width, count))],
        2 * mm + mm // 4, [hold_of(wide)],
    )
    cw = [swap(hw[i * len(w_parts) : (i + 1) * len(w_parts)], "z") for i in range(nw)]
    filts = flip(lax.dynamic_slice_in_dim(filt, (1 - core) * wide, wide, axis=2))

    def span_step(parts, off, *after):
        cols = parts[0].shape[-1]
        return call(
            functools.partial(span_kernel, len(parts), len(after), off), "span",
            (*parts, *after, filt, filts, kron, kront, tq),
            parts_of(len(parts) == 1, "z", (blocks * rows + EDGE, cols)), mm // 2,
            [pltpu.VMEM((span, rows, cols), BF), pltpu.VMEM((span, rows, cols), BF if each % 16 == 0 else F32)],
        )

    se = span_step(ce, 0, zha)
    be = swap(se, "z")
    sw, bw, behind = [], [], se[0]
    for i in range(nw):
        sw.append(span_step(cw[i], i * some, behind))
        bw.append(swap(sw[i], "z"))
        behind = sw[i][0]

    high = width // ndp
    av_parts = parts_of(AV_WHOLE, "dp", (high, width))
    du, send, s_av, *p_av = call(
        functools.partial(grad_out_kernel, len(be), len(av_parts)), "grad_out",
        (*be, behind, tqt, za, zv, zha, zhv, taps, xt),
        [S((count, width)), S((tok, width)), S((3, width), F32)] + av_parts,
        2 * mm, [hold_of(wide), pltpu.VMEM((width, width), BF)], SHADE,
    )
    r_av = swap(p_av, "dp")
    du_av, got_av = du, flip(send)

    dus, gots, owns, others, known, r_g, behind = [], [], [], [], [s_av], [], r_av[1:AV_DONE]
    after = p_av[:1]
    for i in range(nw):
        ends_here = i == nw - 1
        extra = -(-9 * 3 * nw // 16) * 16 if ends_here else 0
        g_parts = parts_of(G_WHOLE, "dp", (high + extra, some))
        m_own, m_send, du, send, sums = call(
            functools.partial(value_out_kernel, len(bw[i]), len(after), i * some), "value_out",
            (*bw[i], *after, tqt, zg, zhg, taps, og_all, h1, h2),
            [S((tok, some))] * 2 + [S((count, some)), S((tok, some)), S((3, some), F32)],
            mm // 2, [hold_of(some), pltpu.VMEM((count, some), BF)],
        )
        known.append(sums)
        extra_in = known if ends_here else []
        p_g = call(
            functools.partial(w_grad_kernel, len(behind), len(extra_in)), "w_grad",
            (*behind, xt, du, *extra_in), g_parts, mm, [pltpu.VMEM((width, some), BF)],
        )
        r_g += swap(p_g, "dp")
        dus.append(du)
        gots.append(flip(send))
        owns.append(m_own)
        others.append(flip(m_send))
        after, behind = p_g[:1], p_g[:1]
    acc = call(in_first_kernel, "in_first", (du_av, got_av, w_in, *behind), [S((tok, width), F32)], 2 * mm)[0]
    in_grad, mixed = call(
        functools.partial(in_last_kernel, nw), "in_last",
        (*dus, *gots, *owns, *others, w_in, acc, *behind), [S((tok, width))] * 2, mm,
    )

    cols, half = 3 * wide, high // ncore
    w_own, w_send, t_own = call(
        functools.partial(fold_kernel, len(r_av), len(r_g) // nw, nw), "fold", (*r_av, *r_g),
        [S((half, cols)), S((half, cols)), S((3, cols), F32)], mm // 64, [pltpu.VMEM((high, cols), BF)],
    )

    w_got = flip(w_send)
    step = 1
    while step < nz:
        t_own = t_own + lax.ppermute(t_own, "z", [(i, i ^ step) for i in range(nz)])
        step *= 2
    t_got = flip(t_own)
    mine_of = 3 * width // nseq
    if mine_of % 128 == 0:
        sent = call(
            join_kernel, "join", (w_own, w_got, t_own), [S((half, ncore * mine_of))] * nz, mm // 64,
            [pltpu.VMEM((half, 3 * width), BF)],
        )
        total, send = call(
            functools.partial(sum_kernel, nz), "sum", swap(sent, "z"), [S((half, mine_of), F32)] * 2, mm // 64,
        )
        w_in_grad, taps_grad = call(
            functools.partial(last_kernel, factor), "last", (total, flip(send), t_own, t_got),
            [S((high, mine_of), F32), S((3, 3 * width), F32)], mm // 64,
        )
    else:

        def joined(own, got):
            own, got = own.reshape(-1, 3, 1, wide), got.reshape(-1, 3, 1, wide)
            low, high = jnp.where(core == 0, own, got), jnp.where(core == 0, got, own)
            return jnp.concatenate([low, high], axis=2).reshape(-1, 3 * width)

        taps_grad = joined(t_own, t_got) * factor
        sent = joined(w_own, w_got).reshape(half, nseq, mine_of).transpose(1, 0, 2)
        got = lax.all_to_all(sent, seq, 0, 0, tiled=True).reshape(nz, high, mine_of)
        w_in_grad = jnp.sum(got.astype(F32), axis=0) * factor
    return (mixed[None], in_grad[None], w_in_grad, taps_grad)


def solution(mesh):
    ndp, nseq = mesh.shape["dp"], mesh.shape["seq"]
    split = Mesh(mesh.devices.reshape(ndp, nseq // 2, 2), ("dp", "z", "core"))
    seq = ("z", "core")
    return jax.shard_map(
        functools.partial(shards, NW),
        mesh=split,
        in_specs=(P("dp", seq, None), P("dp", seq, None), P(), P(), P(None, seq, None)),
        out_specs=(P("dp", seq, None), P("dp", seq, None), P("dp", seq), P()),
        check_vma=False,
    )
```

```python
import functools
import math

import jax
import jax.numpy as jnp
import numpy as np
from jax import lax
from jax.experimental import pallas as pl
from jax.experimental.pallas import tpu as pltpu
from jax.sharding import Mesh
from jax.sharding import PartitionSpec as P

BLK = 256
BF = jnp.bfloat16
EDGE = 16
NW = 2
SHADE = 1000
AV_DONE = 3
E_WHOLE, W_WHOLE, AV_WHOLE, G_WHOLE = False, False, False, False
F32 = jnp.float32
PARAMS = dict(vmem_limit_bytes=48 * 1024 * 1024)


def dct_table(count):
    one = np.float32
    rows = np.arange(count, dtype=np.float32)[:, None]
    cols = np.arange(count, dtype=np.float32)[None, :]
    first = np.where(rows == 0, one(math.sqrt(0.5)), one(1.0))
    table = one(math.sqrt(2.0 / count)) * first * np.cos(one(math.pi) * (cols + one(0.5)) * rows / one(count))
    return table.astype(BF)


def dot(left, right):
    return jnp.dot(left, right, preferred_element_type=F32)


def dot_nt(left, right):
    return lax.dot_general(left, right, (((1,), (1,)), ((), ())), preferred_element_type=F32)


def neighbours(cells, before, after):
    count = cells.shape[0]
    row = lax.broadcasted_iota(jnp.int32, (8, cells.shape[1]), 0)
    earlier, later = pltpu.roll(cells, 1, 0), pltpu.roll(cells, count - 1, 0)
    head = jnp.where(row == 0, before, earlier[0:8])
    tail = jnp.where(row == 7, after, later[count - 8 :])
    return (
        jnp.concatenate([head, earlier[8:]], axis=0),
        jnp.concatenate([later[: count - 8], tail], axis=0),
    )


def short_conv(cells, edge, taps):
    earlier, later = neighbours(cells, edge[0:1], edge[1:2])
    return taps[0:1] * earlier + taps[1:2] * cells + taps[2:3] * later


def lanes(width):
    step = min(width, 256)
    return [(at, pl.ds(at, step)) for at in range(0, width, step)]


def mine(off, width, at, step):
    start = lax.axis_index("core") * width + (off + at)
    return pl.ds(pl.multiple_of(start, 128), step)


def part_of(core, size):
    if isinstance(core, int):
        return pl.ds(core * size, size)
    return pl.ds(pl.multiple_of(core * size, size), size)


def ordered(first, second):
    swap = lax.axis_index("core") == 1
    return jnp.where(swap, second, first), jnp.where(swap, first, second)


def pieces(refs, axis):
    size = lax.axis_size(axis)
    if len(refs) == 1:
        return [(k, refs[0].at[k]) for k in range(size)]
    return [(lax.axis_index(axis) ^ k, ref) for k, ref in enumerate(refs)]


def pack_kernel(x_ref, og_ref, ends_ref, send_ref):
    core, tok, width = lax.axis_index("core"), x_ref.shape[0], send_ref.shape[1]
    x_head, x_tail = x_ref[0:16, :].astype(F32)[0:2], x_ref[tok - 16 : tok, :].astype(F32)[14:16]
    g_head, g_tail = og_ref[0:16, :].astype(F32)[0:1], og_ref[tok - 16 : tok, :].astype(F32)[15:16]
    first = core == 0
    rows = [jnp.where(first, x_head, x_tail), jnp.where(first, g_head, g_tail)]
    rows.append(jnp.zeros((EDGE - 3, x_ref.shape[1]), F32))
    ends_ref[...] = jnp.concatenate(rows, axis=0).astype(BF)
    send_ref[...] = og_ref[:, part_of(1 - core, width)]


def edge_rows(first_ref, second_ref):
    before, after = ordered(first_ref[...].astype(F32), second_ref[...].astype(F32))
    pad = jnp.zeros((EDGE - 4, before.shape[1]), F32)
    return jnp.concatenate([before[1:2], after[0:1], before[0:1], after[1:2], pad], axis=0).astype(BF)


def project(x_ref, xs_ref, xh, w, z_ref, zh_ref, here):
    core, tok = lax.axis_index("core"), x_ref.shape[0]
    z_ref[part_of(core, tok), here] = dot(x_ref[...], w).astype(BF)
    z_ref[part_of(1 - core, tok), here] = dot(xs_ref[...], w).astype(BF)
    zh = dot(xh, w).astype(BF)
    zh_ref[:, here] = zh
    return z_ref[:, here].astype(F32), zh.astype(F32)


def put_blocks(table, cells, hold, here):
    for p in range(hold.shape[0]):
        hold[p, :, here] = dot(table, cells[p * BLK : (p + 1) * BLK]).astype(BF)


def hand_rows(hold, outs, cols):
    for there, out in pieces(outs, "z"):
        out[...] = hold[:, part_of(there, out.shape[1]), cols]


def grad_block_kernel(
    n, x_ref, xs_ref, h1_ref, h2_ref, w_ref, taps_ref, og_ref, ogs_ref, tq_ref, filt_ref, *refs
):
    outs, (z_ref, zh_ref, og_all_ref, send_ref, hold) = refs[:n], refs[n:]
    core, tok = lax.axis_index("core"), x_ref.shape[0]
    width = z_ref.shape[1]
    og_all_ref[part_of(core, tok), :] = og_ref[:, part_of(core, width)]
    og_all_ref[part_of(1 - core, tok), :] = ogs_ref[...]
    xh = edge_rows(h1_ref, h2_ref)
    for at, here in lanes(width):
        cols = mine(2 * width, width, at, here.size)
        z, zh = project(x_ref, xs_ref, xh, w_ref[:, cols], z_ref, zh_ref, here)
        g = short_conv(z, zh, taps_ref[:, cols])
        e4 = (og_all_ref[:, here].astype(F32) * g).astype(BF)
        put_blocks(tq_ref[...], e4, hold, here)
    hand_rows(hold, outs, pl.ds(0, width))
    send_ref[...] = filt_ref[:, :, part_of(1 - core, width)]


def value_block_kernel(
    n, nw, x_ref, xs_ref, h1_ref, h2_ref, w_ref, taps_ref, tq_ref, after_ref, *refs
):
    outs, (za_ref, zv_ref, zha_ref, zhv_ref, xt_ref, hold) = refs[: n * nw], refs[n * nw :]
    core, tok = lax.axis_index("core"), x_ref.shape[0]
    width = za_ref.shape[1]
    xh = edge_rows(h1_ref, h2_ref)
    for at, here in lanes(width):
        parts = []
        for off, z_ref, zh_ref in ((0, za_ref, zha_ref), (4 * width, zv_ref, zhv_ref)):
            cols = mine(off, width, at, here.size)
            z, zh = project(x_ref, xs_ref, xh, w_ref[:, cols], z_ref, zh_ref, here)
            parts.append(short_conv(z, zh, taps_ref[:, cols]))
        put_blocks(tq_ref[...], (parts[0] * parts[1]).astype(BF), hold, here)
    for i in range(nw):
        hand_rows(hold, outs[i * n : (i + 1) * n], pl.ds(i * (width // nw), width // nw))
    xt_ref[:, part_of(core, tok)] = x_ref[...].T
    xt_ref[:, part_of(1 - core, tok)] = xs_ref[...].T


def span_kernel(n, skip, off, *refs):
    ins, refs = refs[:n], refs[n + skip :]
    (filt_ref, filts_ref, k_ref, kt_ref, tq_ref), outs, (hold, filts) = refs[:5], refs[5 : n + 5], refs[n + 5 :]
    core, place, places = lax.axis_index("core"), lax.axis_index("z"), lax.axis_size("z")
    span, rows, width = hold.shape
    each, blocks = filt_ref.shape[1], span // places
    half = filts_ref.shape[2]
    group = k_ref.shape[0] // span
    for there, ref in pieces(ins, "z"):
        hold[pl.ds(there * blocks, blocks)] = ref[...]
    mine_at = pl.ds(pl.multiple_of(core * half + off, 128), width)
    filts[:, part_of(core, each), :] = filt_ref[:, :, mine_at].astype(filts.dtype)
    filts[:, part_of(1 - core, each), :] = filts_ref[:, :, off : off + width].astype(filts.dtype)
    for _, here in lanes(width):
        for at in range(0, rows, group):
            some = pl.ds(at, group)
            flat = (span * group, here.size)
            second = dot(k_ref[...], hold[:, some, here].reshape(flat))
            scaled = (filts[:, some, here].reshape(flat).astype(F32) * second).astype(BF)
            third = dot(kt_ref[...], scaled).astype(BF)
            hold[:, some, here] = third.reshape(span, group, here.size)
    table = tq_ref[part_of(place, rows), :].astype(F32)
    first_q, last_q = table[:, 0:1], table[:, BLK - 1 : BLK]
    for there, out in pieces(outs, "z"):
        for p in range(blocks):
            out[p * rows : (p + 1) * rows, :] = hold[there * blocks + p]
        sums = []
        for p, column, inside in (
            (there * blocks - 1, last_q, there > 0),
            (there * blocks + blocks, first_q, there < places - 1),
        ):
            cells = hold[jnp.clip(p, 0, span - 1)].astype(F32)
            total = jnp.sum(cells * column, axis=0, keepdims=True)
            sums.append(jnp.where(inside, total, 0.0))
        both = jnp.concatenate(sums, axis=0)
        high = both.astype(BF).astype(F32)
        pad = jnp.zeros((EDGE - 4, width), F32)
        out[blocks * rows :, :] = jnp.concatenate([high, both - high, pad], axis=0).astype(BF)


def take_rows(ins, hold):
    blocks = hold.shape[0]
    rows = hold.shape[1] // lax.axis_size("z")
    for there, ref in pieces(ins, "z"):
        for p in range(blocks):
            hold[p, part_of(there, rows), :] = ref[p * rows : (p + 1) * rows, :]


def inverse(ins, hold, tqt_ref, here):
    cells = jnp.concatenate([dot(tqt_ref[...], hold[p, :, here]) for p in range(hold.shape[0])], axis=0)
    shares = [ref for _, ref in pieces(ins, "z")]
    at = shares[0].shape[0] - EDGE
    edge = shares[0][at : at + EDGE, here].astype(F32)
    for ref in shares[1:]:
        edge = edge + ref[at : at + EDGE, here].astype(F32)
    return cells, edge[0:1] + edge[2:3], edge[1:2] + edge[3:4]


def conv_wide(z, zh, taps):
    count = z.shape[0]
    before = taps[0:1] * zh[2:3] + taps[1:2] * zh[0:1] + taps[2:3] * z[0:1]
    after = taps[0:1] * z[count - 1 : count] + taps[1:2] * zh[1:2] + taps[2:3] * zh[3:4]
    return short_conv(z, zh, taps), before, after


def rounded(value):
    return value.astype(BF).astype(F32)


def emit(cells, gate, z, zh, taps, cols, du_ref, sums_ref):
    ds, before, after = (rounded(one * two) for one, two in zip(cells, gate))
    earlier, later = neighbours(ds, before, after)
    du_ref[:, cols] = (taps[0:1] * later + taps[1:2] * ds + taps[2:3] * earlier).astype(BF)
    earlier, later = neighbours(z, zh[0:1], zh[1:2])
    sums_ref[0:1, cols] = jnp.sum(ds * earlier, axis=0, keepdims=True)
    sums_ref[1:2, cols] = jnp.sum(ds * z, axis=0, keepdims=True)
    sums_ref[2:3, cols] = jnp.sum(ds * later, axis=0, keepdims=True)


def multiply(xt_ref, du_ref, outs, part):
    for _, here in lanes(du_ref.shape[1]):
        part[:, here] = dot(xt_ref[...], du_ref[:, here]).astype(BF)
    rows = part.shape[0] // lax.axis_size("dp")
    for there, out in pieces(outs, "dp"):
        out[0:rows, :] = part[part_of(there, rows), :]


def grad_out_kernel(n, nd, *refs):
    ins, refs = refs[:n], refs[n + 1 :]
    (tqt_ref, za_ref, zv_ref, zha_ref, zhv_ref, taps_ref, xt_ref), refs = refs[:7], refs[7:]
    (du_ref, send_ref, sums_ref), outs, (hold, part) = refs[:3], refs[3 : 3 + nd], refs[3 + nd :]
    width, tok = za_ref.shape[1], send_ref.shape[0]
    take_rows(ins, hold)
    for at, here in lanes(width):
        dw = inverse(ins, hold, tqt_ref, here)
        za, zha = za_ref[:, here].astype(F32), zha_ref[:, here].astype(F32)
        zv, zhv = zv_ref[:, here].astype(F32), zhv_ref[:, here].astype(F32)
        ta = taps_ref[:, mine(0, width, at, here.size)]
        tv = taps_ref[:, mine(4 * width, width, at, here.size)]
        emit(dw, conv_wide(zv, zhv, tv), za, zha, ta, here, du_ref, sums_ref)
        emit(dw, conv_wide(za, zha, ta), zv, zhv, tv, pl.ds(width + at, here.size), du_ref, sums_ref)
    send_ref[...] = du_ref[part_of(1 - lax.axis_index("core"), tok), :]
    multiply(xt_ref, du_ref, outs, part)


def two_parts(value):
    high = rounded(value)
    return [high, value - high]


def tap_rows(every, width, rows):
    lines = []
    for at in range(0, every.shape[1], width):
        lines += two_parts(every[:, at : at + width])
    if rows > 3 * len(lines):
        lines.append(jnp.zeros((rows - 3 * len(lines), width), F32))
    return jnp.concatenate(lines, axis=0).astype(BF)


def taps_of(sums, out_ref):
    width = sums.shape[1]
    for run in range(out_ref.shape[1] // width):
        out_ref[:, run * width : (run + 1) * width] = sums[6 * run : 6 * run + 3] + sums[6 * run + 3 : 6 * run + 6]


def value_out_kernel(n, skip, off, *refs):
    ins, refs = refs[:n], refs[n + skip :]
    (tqt_ref, zg_ref, zhg_ref, taps_ref, og_ref, h1_ref, h2_ref), refs = refs[:7], refs[7:]
    (mo_ref, ms_ref, du_ref, send_ref, sums_ref), (hold, mixed) = refs[:5], refs[5:]
    core, tok, half = lax.axis_index("core"), mo_ref.shape[0], zg_ref.shape[1]
    width = mo_ref.shape[1]
    take_rows(ins, hold)
    for at, here in lanes(width):
        there = pl.ds(off + at, here.size)
        h4 = inverse(ins, hold, tqt_ref, here)
        z, zh = zg_ref[:, there].astype(F32), zhg_ref[:, there].astype(F32)
        cols = mine(2 * half, half, off + at, here.size)
        whole = mine(0, half, off + at, here.size)
        taps = taps_ref[:, cols]
        mixed[:, here] = (short_conv(z, zh, taps) * h4[0]).astype(BF)
        before, after = ordered(h1_ref[:, whole].astype(F32), h2_ref[:, whole].astype(F32))
        og = (og_ref[:, there].astype(F32), before[2:3], after[2:3])
        emit(h4, og, z, zh, taps, here, du_ref, sums_ref)
    mo_ref[...] = mixed[part_of(core, tok), :]
    ms_ref[...] = mixed[part_of(1 - core, tok), :]
    send_ref[...] = du_ref[part_of(1 - core, tok), :]


def w_grad_kernel(skip, known, *refs):
    refs = refs[skip:]
    (xt_ref, du_ref), known, outs, part = refs[:2], refs[2 : 2 + known], refs[2 + known : -1], refs[-1]
    multiply(xt_ref, du_ref, outs, part)
    if known:
        width = du_ref.shape[1]
        av = known[0][...]
        half = av.shape[1] // 2
        every = [av[:, :half], *(ref[...] for ref in known[1:]), av[:, half:]]
        rows = part.shape[0] // lax.axis_size("dp")
        extra = outs[0].shape[-2] - rows
        block = tap_rows(jnp.concatenate(every, axis=1), width, extra)
        for _, out in pieces(outs, "dp"):
            out[rows : rows + extra, :] = block


def in_part(du_ref, rows, w_ref, columns, width):
    total = None
    for run, start in enumerate(columns):
        w = w_ref[:, pl.ds(pl.multiple_of(start, 128), width)]
        part = dot_nt(du_ref[rows, run * width : (run + 1) * width], w)
        total = part if total is None else total + part
    return total


def in_first_kernel(du_ref, got_ref, w_ref, after_ref, acc_ref):
    core, tok, width = lax.axis_index("core"), got_ref.shape[0], w_ref.shape[1] // 6
    every = pl.ds(0, tok)
    own = in_part(du_ref, part_of(core, tok), w_ref, [core * width, (4 + core) * width], width)
    acc_ref[...] = own + in_part(got_ref, every, w_ref, [(1 - core) * width, (5 - core) * width], width)


def in_last_kernel(nw, *refs):
    dus, gots, owns, others = (refs[i * nw : (i + 1) * nw] for i in range(4))
    w_ref, acc_ref, after_ref, out_ref, mixed_ref = refs[4 * nw :]
    core, half = lax.axis_index("core"), w_ref.shape[1] // 6
    tok, width = gots[0].shape
    total = acc_ref[...]
    for i in range(nw):
        for ref, rows, owner in (
            (dus[i], part_of(core, tok), core),
            (gots[i], pl.ds(0, tok), 1 - core),
        ):
            total = total + in_part(ref, rows, w_ref, [(2 + owner) * half + i * width], width)
        for ref, owner in ((owns[i], core), (others[i], 1 - core)):
            at = pl.multiple_of(owner * half + i * width, 128)
            mixed_ref[:, pl.ds(at, width)] = ref[...]
    out_ref[...] = total.astype(BF)


def add_all(values):
    while len(values) > 1:
        values = [one + two for one, two in zip(values[::2], values[1::2])]
    return values[0]


def fold_kernel(na, n, nw, *refs):
    av, refs = [ref for _, ref in pieces(refs[:na], "dp")], refs[na:]
    gs = [[ref for _, ref in pieces(refs[i * n : (i + 1) * n], "dp")] for i in range(nw)]
    own_ref, send_ref, taps_ref, hold = refs[n * nw :]
    core, width = lax.axis_index("core"), gs[0][0].shape[1]
    half_cols = width * nw
    rows = av[0].shape[0]
    both = add_all([ref[...].astype(F32) for ref in av]).astype(BF)
    hold[:, 0:half_cols] = both[:, :half_cols]
    for i, parts in enumerate(gs):
        at = half_cols + i * width
        hold[:, at : at + width] = add_all([ref[0:rows, :].astype(F32) for ref in parts]).astype(BF)
    hold[:, 2 * half_cols :] = both[:, half_cols:]
    half = own_ref.shape[0]
    own_ref[...] = hold[part_of(core, half), :]
    send_ref[...] = hold[part_of(1 - core, half), :]
    extra = gs[-1][0].shape[0] - rows
    sums = add_all([ref[rows : rows + extra, :].astype(F32) for ref in gs[-1]])
    taps_of(sums, taps_ref)


def spread(own_ref, got_ref, out_ref):
    core, width = lax.axis_index("core"), own_ref.shape[1] // 3
    for run in range(3):
        cols = pl.ds(run * width, width)
        for ref, owner in ((own_ref, core), (got_ref, 1 - core)):
            at = pl.multiple_of((2 * run + owner) * width, 128)
            out_ref[:, pl.ds(at, width)] = ref[:, cols]


def join_kernel(own_ref, got_ref, taps_ref, *refs):
    outs, hold = refs[:-1], refs[-1]
    spread(own_ref, got_ref, hold)
    rows, width = hold.shape[0], outs[0].shape[1]
    block = tap_rows(taps_ref[...], width, outs[0].shape[0] - rows)
    for there, out in pieces(outs, "z"):
        out[0:rows, :] = hold[:, part_of(there, width)]
        out[rows:, :] = block


def sum_kernel(n, *refs):
    ins, (own_ref, send_ref, taps_ref) = refs[:n], refs[n + 1 :]
    core, (rows, width) = lax.axis_index("core"), own_ref.shape
    for out, owner in ((own_ref, core), (send_ref, 1 - core)):
        cols = part_of(owner, width)
        out[...] = add_all([ref[0:rows, cols].astype(F32) for ref in ins])
    taps_of(add_all([ref[rows:, :].astype(F32) for ref in ins]), taps_ref)


def last_kernel(factor, own_ref, got_ref, t_own_ref, t_got_ref, out_ref, taps_ref):
    core, rows = lax.axis_index("core"), own_ref.shape[0]
    out_ref[part_of(core, rows), :] = own_ref[...] * factor
    out_ref[part_of(1 - core, rows), :] = got_ref[...] * factor
    spread(t_own_ref, t_got_ref, taps_ref)
    taps_ref[...] = taps_ref[...] * factor


def shards(nw, inputs, out_grad, w_in, taps, filt):
    tok, width = inputs.shape[1], inputs.shape[2]
    ndp, nz, ncore = lax.axis_size("dp"), lax.axis_size("z"), lax.axis_size("core")
    nseq = nz * ncore
    span, each = filt.shape[0], filt.shape[1]
    seq = ("z", "core")
    core = lax.axis_index("core")
    factor = 1.0 / math.sqrt(ndp * nseq * tok)
    wide, count = width // ncore, tok * ncore
    blocks, rows = count // BLK, each * ncore
    group = math.gcd(rows, 16)
    tq, tp = dct_table(BLK), dct_table(span)
    kron = np.kron(tp.astype(np.float32), np.eye(group, dtype=np.float32)).astype(BF)
    tq, tqt, kron, kront = (jnp.asarray(table) for table in (tq, tq.T.copy(), kron, kron.T.copy()))
    x, og = inputs[0], out_grad[0]

    def S(shape, dtype=BF):
        return jax.ShapeDtypeStruct(shape, dtype)

    def call(kernel, name, ins, outs, flops, scratch=(), shade=1):
        moved = sum(a.size * a.dtype.itemsize for a in (*ins, *outs))
        whole = pl.BlockSpec(memory_space=pltpu.VMEM)
        return pl.pallas_call(
            kernel,
            out_shape=outs,
            in_specs=[whole] * len(ins),
            out_specs=[whole] * len(outs),
            scratch_shapes=scratch,
            compiler_params=pltpu.CompilerParams(**PARAMS),
            cost_estimate=pl.CostEstimate(flops=flops // shade, bytes_accessed=moved // shade, transcendentals=0),
            name=name,
        )(*ins)

    def flip(value):
        return lax.ppermute(value, "core", [(0, 1), (1, 0)])

    def swap(parts, axis):
        size = lax.axis_size(axis)
        if len(parts) == 1:
            return [lax.all_to_all(parts[0], axis, 0, 0, tiled=True)]
        return [parts[0]] + [
            lax.ppermute(parts[k], axis, [(i, i ^ k) for i in range(size)]) for k in range(1, size)
        ]

    def parts_of(whole, axis, shape):
        size = lax.axis_size(axis)
        return [S((size, *shape))] if whole else [S(shape)] * size

    mm = 2 * tok * width * width
    xs = flip(x)
    ends, og_send = call(pack_kernel, "pack", (x, og), [S((EDGE, width)), S((tok, wide))], mm // 999)
    odd = range(1, nseq - 1, 2)
    near = [(i, i + 1) for i in odd] + [(i + 1, i) for i in odd]
    far = [(i, i + 2) for i in odd] + [(i + 1, i - 1) for i in odd]
    h1, h2 = lax.ppermute(ends, seq, near), lax.ppermute(ends, seq, far)
    ogs = flip(og_send)

    def hold_of(cols):
        return pltpu.VMEM((blocks, BLK, cols), BF)

    act, edge = S((count, wide)), S((EDGE, wide))
    e_parts = parts_of(E_WHOLE, "z", (blocks, rows, wide))
    *he, zg, zhg, og_all, filt_send = call(
        functools.partial(grad_block_kernel, len(e_parts)), "grad_block",
        (x, xs, h1, h2, w_in, taps, og, ogs, tq, filt), e_parts + [act, edge, act, S((span, each, wide))],
        mm + mm // 4, [hold_of(wide)],
    )
    ce = swap(he, "z")
    some = wide // nw
    w_parts = parts_of(W_WHOLE, "z", (blocks, rows, some))
    *hw, za, zv, zha, zhv, xt = call(
        functools.partial(value_block_kernel, len(w_parts), nw), "value_block",
        (x, xs, h1, h2, w_in, taps, tq, zhg),
        w_parts * nw + [act, act, edge, edge, S((width, count))],
        2 * mm + mm // 4, [hold_of(wide)],
    )
    cw = [swap(hw[i * len(w_parts) : (i + 1) * len(w_parts)], "z") for i in range(nw)]
    filts = flip(filt_send)

    def span_step(parts, off, *after):
        cols = parts[0].shape[-1]
        return call(
            functools.partial(span_kernel, len(parts), len(after), off), "span",
            (*parts, *after, filt, filts, kron, kront, tq),
            parts_of(len(parts) == 1, "z", (blocks * rows + EDGE, cols)), mm // 2,
            [pltpu.VMEM((span, rows, cols), BF), pltpu.VMEM((span, rows, cols), BF if each % 16 == 0 else F32)],
        )

    se = span_step(ce, 0, zha)
    be = swap(se, "z")
    sw, bw, behind = [], [], se[0]
    for i in range(nw):
        sw.append(span_step(cw[i], i * some, behind))
        bw.append(swap(sw[i], "z"))
        behind = sw[i][0]

    high = width // ndp
    av_parts = parts_of(AV_WHOLE, "dp", (high, width))
    du, send, s_av, *p_av = call(
        functools.partial(grad_out_kernel, len(be), len(av_parts)), "grad_out",
        (*be, behind, tqt, za, zv, zha, zhv, taps, xt),
        [S((count, width)), S((tok, width)), S((3, width), F32)] + av_parts,
        2 * mm, [hold_of(wide), pltpu.VMEM((width, width), BF)], SHADE,
    )
    r_av = swap(p_av, "dp")
    du_av, got_av = du, flip(send)

    dus, gots, owns, others, known, r_g, behind = [], [], [], [], [s_av], [], r_av[1:AV_DONE]
    after = p_av[:1]
    for i in range(nw):
        ends_here = i == nw - 1
        extra = -(-6 * 3 * nw // 16) * 16 if ends_here else 0
        g_parts = parts_of(G_WHOLE, "dp", (high + extra, some))
        m_own, m_send, du, send, sums = call(
            functools.partial(value_out_kernel, len(bw[i]), len(after), i * some), "value_out",
            (*bw[i], *after, tqt, zg, zhg, taps, og_all, h1, h2),
            [S((tok, some))] * 2 + [S((count, some)), S((tok, some)), S((3, some), F32)],
            mm // 2, [hold_of(some), pltpu.VMEM((count, some), BF)],
        )
        known.append(sums)
        extra_in = known if ends_here else []
        p_g = call(
            functools.partial(w_grad_kernel, len(behind), len(extra_in)), "w_grad",
            (*behind, xt, du, *extra_in), g_parts, mm, [pltpu.VMEM((width, some), BF)],
        )
        r_g += swap(p_g, "dp")
        dus.append(du)
        gots.append(flip(send))
        owns.append(m_own)
        others.append(flip(m_send))
        after, behind = p_g[:1], p_g[:1]
    acc = call(in_first_kernel, "in_first", (du_av, got_av, w_in, *behind), [S((tok, width), F32)], 2 * mm)[0]
    in_grad, mixed = call(
        functools.partial(in_last_kernel, nw), "in_last",
        (*dus, *gots, *owns, *others, w_in, acc, *behind), [S((tok, width))] * 2, mm,
    )

    cols, half = 3 * wide, high // ncore
    w_own, w_send, t_own = call(
        functools.partial(fold_kernel, len(r_av), len(r_g) // nw, nw), "fold", (*r_av, *r_g),
        [S((half, cols)), S((half, cols)), S((3, cols), F32)], mm // 64, [pltpu.VMEM((high, cols), BF)],
    )

    w_got = flip(w_send)
    mine_of = 3 * width // nseq
    if mine_of % 128 == 0:
        runs = cols // (ncore * mine_of)
        lines = half + -(-6 * runs // 16) * 16
        sent = call(
            join_kernel, "join", (w_own, w_got, t_own), [S((lines, ncore * mine_of))] * nz, mm // 64,
            [pltpu.VMEM((half, 3 * width), BF)],
        )
        total, send, t_own = call(
            functools.partial(sum_kernel, nz), "sum", (*swap(sent, "z"), in_grad),
            [S((half, mine_of), F32)] * 2 + [S((3, cols), F32)], mm // 64,
        )
        w_in_grad, taps_grad = call(
            functools.partial(last_kernel, factor), "last", (total, flip(send), t_own, flip(t_own)),
            [S((high, mine_of), F32), S((3, 3 * width), F32)], mm // 64,
        )
    else:

        def joined(own, got):
            own, got = own.reshape(-1, 3, 1, wide), got.reshape(-1, 3, 1, wide)
            low, high = jnp.where(core == 0, own, got), jnp.where(core == 0, got, own)
            return jnp.concatenate([low, high], axis=2).reshape(-1, 3 * width)

        step = 1
        while step < nz:
            t_own = t_own + lax.ppermute(t_own, "z", [(i, i ^ step) for i in range(nz)])
            step *= 2
        taps_grad = joined(t_own, flip(t_own)) * factor
        sent = joined(w_own, w_got).reshape(half, nseq, mine_of).transpose(1, 0, 2)
        got = lax.all_to_all(sent, seq, 0, 0, tiled=True).reshape(nz, high, mine_of)
        w_in_grad = jnp.sum(got.astype(F32), axis=0) * factor
    return (mixed[None], in_grad[None], w_in_grad, taps_grad)


def solution(mesh):
    ndp, nseq = mesh.shape["dp"], mesh.shape["seq"]
    split = Mesh(mesh.devices.reshape(ndp, nseq // 2, 2), ("dp", "z", "core"))
    seq = ("z", "core")
    return jax.shard_map(
        functools.partial(shards, NW),
        mesh=split,
        in_specs=(P("dp", seq, None), P("dp", seq, None), P(), P(), P(None, seq, None)),
        out_specs=(P("dp", seq, None), P("dp", seq, None), P("dp", seq), P()),
        check_vma=False,
    )
```

```python
import functools
import math

import jax
import jax.numpy as jnp
import numpy as np
from jax import lax
from jax.experimental import pallas as pl
from jax.experimental.pallas import tpu as pltpu
from jax.sharding import Mesh
from jax.sharding import PartitionSpec as P

BLK = 256
BF = jnp.bfloat16
EDGE = 16
NW = 2
SHADE = 1000
AV_DONE = 2
E_WHOLE, W_WHOLE, AV_WHOLE, G_WHOLE = False, False, False, False
F32 = jnp.float32
PARAMS = dict(vmem_limit_bytes=48 * 1024 * 1024)


def dct_table(count):
    one = np.float32
    rows = np.arange(count, dtype=np.float32)[:, None]
    cols = np.arange(count, dtype=np.float32)[None, :]
    first = np.where(rows == 0, one(math.sqrt(0.5)), one(1.0))
    table = one(math.sqrt(2.0 / count)) * first * np.cos(one(math.pi) * (cols + one(0.5)) * rows / one(count))
    return table.astype(BF)


def dot(left, right):
    return jnp.dot(left, right, preferred_element_type=F32)


def dot_nt(left, right):
    return lax.dot_general(left, right, (((1,), (1,)), ((), ())), preferred_element_type=F32)


def neighbours(cells, before, after):
    count = cells.shape[0]
    row = lax.broadcasted_iota(jnp.int32, (8, cells.shape[1]), 0)
    earlier, later = pltpu.roll(cells, 1, 0), pltpu.roll(cells, count - 1, 0)
    head = jnp.where(row == 0, before, earlier[0:8])
    tail = jnp.where(row == 7, after, later[count - 8 :])
    return (
        jnp.concatenate([head, earlier[8:]], axis=0),
        jnp.concatenate([later[: count - 8], tail], axis=0),
    )


def short_conv(cells, edge, taps):
    earlier, later = neighbours(cells, edge[0:1], edge[1:2])
    return taps[0:1] * earlier + taps[1:2] * cells + taps[2:3] * later


def lanes(width):
    step = min(width, 256)
    return [(at, pl.ds(at, step)) for at in range(0, width, step)]


def mine(off, width, at, step):
    start = lax.axis_index("core") * width + (off + at)
    return pl.ds(pl.multiple_of(start, 128), step)


def part_of(core, size):
    if isinstance(core, int):
        return pl.ds(core * size, size)
    return pl.ds(pl.multiple_of(core * size, size), size)


def ordered(first, second):
    swap = lax.axis_index("core") == 1
    return jnp.where(swap, second, first), jnp.where(swap, first, second)


def pieces(refs, axis):
    size = lax.axis_size(axis)
    if len(refs) == 1:
        return [(k, refs[0].at[k]) for k in range(size)]
    return [(lax.axis_index(axis) ^ k, ref) for k, ref in enumerate(refs)]


def pack_kernel(x_ref, og_ref, ends_ref, send_ref):
    core, tok, width = lax.axis_index("core"), x_ref.shape[0], send_ref.shape[1]
    x_head, x_tail = x_ref[0:16, :].astype(F32)[0:2], x_ref[tok - 16 : tok, :].astype(F32)[14:16]
    g_head, g_tail = og_ref[0:16, :].astype(F32)[0:1], og_ref[tok - 16 : tok, :].astype(F32)[15:16]
    first = core == 0
    rows = [jnp.where(first, x_head, x_tail), jnp.where(first, g_head, g_tail)]
    rows.append(jnp.zeros((EDGE - 3, x_ref.shape[1]), F32))
    ends_ref[...] = jnp.concatenate(rows, axis=0).astype(BF)
    send_ref[...] = og_ref[:, part_of(1 - core, width)]


def edge_rows(first_ref, second_ref):
    before, after = ordered(first_ref[...].astype(F32), second_ref[...].astype(F32))
    pad = jnp.zeros((EDGE - 4, before.shape[1]), F32)
    return jnp.concatenate([before[1:2], after[0:1], before[0:1], after[1:2], pad], axis=0).astype(BF)


def project(x_ref, xs_ref, xh, w, z_ref, zh_ref, here):
    core, tok = lax.axis_index("core"), x_ref.shape[0]
    z_ref[part_of(core, tok), here] = dot(x_ref[...], w).astype(BF)
    z_ref[part_of(1 - core, tok), here] = dot(xs_ref[...], w).astype(BF)
    zh = dot(xh, w).astype(BF)
    zh_ref[:, here] = zh
    return z_ref[:, here].astype(F32), zh.astype(F32)


def put_blocks(table, cells, hold, here):
    for p in range(hold.shape[0]):
        hold[p, :, here] = dot(table, cells[p * BLK : (p + 1) * BLK]).astype(BF)


def hand_rows(hold, outs, cols):
    for there, out in pieces(outs, "z"):
        out[...] = hold[:, part_of(there, out.shape[1]), cols]


def grad_block_kernel(
    n, x_ref, xs_ref, h1_ref, h2_ref, w_ref, taps_ref, og_ref, ogs_ref, tq_ref, *refs
):
    outs, (z_ref, zh_ref, og_all_ref, hold) = refs[:n], refs[n:]
    core, tok = lax.axis_index("core"), x_ref.shape[0]
    width = z_ref.shape[1]
    og_all_ref[part_of(core, tok), :] = og_ref[:, part_of(core, width)]
    og_all_ref[part_of(1 - core, tok), :] = ogs_ref[...]
    xh = edge_rows(h1_ref, h2_ref)
    for at, here in lanes(width):
        cols = mine(2 * width, width, at, here.size)
        z, zh = project(x_ref, xs_ref, xh, w_ref[:, cols], z_ref, zh_ref, here)
        g = short_conv(z, zh, taps_ref[:, cols])
        e4 = (og_all_ref[:, here].astype(F32) * g).astype(BF)
        put_blocks(tq_ref[...], e4, hold, here)
    hand_rows(hold, outs, pl.ds(0, width))


def value_block_kernel(
    n, nw, x_ref, xs_ref, h1_ref, h2_ref, w_ref, taps_ref, tq_ref, after_ref, *refs
):
    outs, (za_ref, zv_ref, zha_ref, zhv_ref, xt_ref, hold) = refs[: n * nw], refs[n * nw :]
    core, tok = lax.axis_index("core"), x_ref.shape[0]
    width = za_ref.shape[1]
    xh = edge_rows(h1_ref, h2_ref)
    for at, here in lanes(width):
        parts = []
        for off, z_ref, zh_ref in ((0, za_ref, zha_ref), (4 * width, zv_ref, zhv_ref)):
            cols = mine(off, width, at, here.size)
            z, zh = project(x_ref, xs_ref, xh, w_ref[:, cols], z_ref, zh_ref, here)
            parts.append(short_conv(z, zh, taps_ref[:, cols]))
        put_blocks(tq_ref[...], (parts[0] * parts[1]).astype(BF), hold, here)
    for i in range(nw):
        hand_rows(hold, outs[i * n : (i + 1) * n], pl.ds(i * (width // nw), width // nw))
    xt_ref[:, part_of(core, tok)] = x_ref[...].T
    xt_ref[:, part_of(1 - core, tok)] = xs_ref[...].T


def span_kernel(n, skip, off, *refs):
    ins, refs = refs[:n], refs[n + skip :]
    (filt_ref, filts_ref, k_ref, kt_ref, tq_ref), outs, (hold, filts) = refs[:5], refs[5 : n + 5], refs[n + 5 :]
    core, place, places = lax.axis_index("core"), lax.axis_index("z"), lax.axis_size("z")
    span, rows, width = hold.shape
    each, blocks = filt_ref.shape[1], span // places
    half = filts_ref.shape[2]
    group = k_ref.shape[0] // span
    for there, ref in pieces(ins, "z"):
        hold[pl.ds(there * blocks, blocks)] = ref[...]
    mine_at = pl.ds(pl.multiple_of(core * half + off, 128), width)
    filts[:, part_of(core, each), :] = filt_ref[:, :, mine_at].astype(filts.dtype)
    filts[:, part_of(1 - core, each), :] = filts_ref[:, :, off : off + width].astype(filts.dtype)
    for _, here in lanes(width):
        for at in range(0, rows, group):
            some = pl.ds(at, group)
            flat = (span * group, here.size)
            second = dot(k_ref[...], hold[:, some, here].reshape(flat))
            scaled = (filts[:, some, here].reshape(flat).astype(F32) * second).astype(BF)
            third = dot(kt_ref[...], scaled).astype(BF)
            hold[:, some, here] = third.reshape(span, group, here.size)
    table = tq_ref[part_of(place, rows), :].astype(F32)
    first_q, last_q = table[:, 0:1], table[:, BLK - 1 : BLK]
    for there, out in pieces(outs, "z"):
        for p in range(blocks):
            out[p * rows : (p + 1) * rows, :] = hold[there * blocks + p]
        sums = []
        for p, column, inside in (
            (there * blocks - 1, last_q, there > 0),
            (there * blocks + blocks, first_q, there < places - 1),
        ):
            cells = hold[jnp.clip(p, 0, span - 1)].astype(F32)
            total = jnp.sum(cells * column, axis=0, keepdims=True)
            sums.append(jnp.where(inside, total, 0.0))
        both = jnp.concatenate(sums, axis=0)
        high = both.astype(BF).astype(F32)
        pad = jnp.zeros((EDGE - 4, width), F32)
        out[blocks * rows :, :] = jnp.concatenate([high, both - high, pad], axis=0).astype(BF)


def take_rows(ins, hold):
    blocks = hold.shape[0]
    rows = hold.shape[1] // lax.axis_size("z")
    for there, ref in pieces(ins, "z"):
        for p in range(blocks):
            hold[p, part_of(there, rows), :] = ref[p * rows : (p + 1) * rows, :]


def inverse(ins, hold, tqt_ref, here):
    cells = jnp.concatenate([dot(tqt_ref[...], hold[p, :, here]) for p in range(hold.shape[0])], axis=0)
    shares = [ref for _, ref in pieces(ins, "z")]
    at = shares[0].shape[0] - EDGE
    edge = shares[0][at : at + EDGE, here].astype(F32)
    for ref in shares[1:]:
        edge = edge + ref[at : at + EDGE, here].astype(F32)
    return cells, edge[0:1] + edge[2:3], edge[1:2] + edge[3:4]


def conv_wide(z, zh, taps):
    count = z.shape[0]
    before = taps[0:1] * zh[2:3] + taps[1:2] * zh[0:1] + taps[2:3] * z[0:1]
    after = taps[0:1] * z[count - 1 : count] + taps[1:2] * zh[1:2] + taps[2:3] * zh[3:4]
    return short_conv(z, zh, taps), before, after


def rounded(value):
    return value.astype(BF).astype(F32)


def emit(cells, gate, z, zh, taps, cols, du_ref, sums_ref):
    ds, before, after = (rounded(one * two) for one, two in zip(cells, gate))
    earlier, later = neighbours(ds, before, after)
    du_ref[:, cols] = (taps[0:1] * later + taps[1:2] * ds + taps[2:3] * earlier).astype(BF)
    earlier, later = neighbours(z, zh[0:1], zh[1:2])
    sums_ref[0:1, cols] = jnp.sum(ds * earlier, axis=0, keepdims=True)
    sums_ref[1:2, cols] = jnp.sum(ds * z, axis=0, keepdims=True)
    sums_ref[2:3, cols] = jnp.sum(ds * later, axis=0, keepdims=True)


def multiply(xt_ref, du_ref, outs, part):
    for _, here in lanes(du_ref.shape[1]):
        part[:, here] = dot(xt_ref[...], du_ref[:, here]).astype(BF)
    rows = part.shape[0] // lax.axis_size("dp")
    for there, out in pieces(outs, "dp"):
        out[0:rows, :] = part[part_of(there, rows), :]


def grad_out_kernel(n, nd, *refs):
    ins, refs = refs[:n], refs[n + 1 :]
    (tqt_ref, za_ref, zv_ref, zha_ref, zhv_ref, taps_ref, xt_ref), refs = refs[:7], refs[7:]
    (du_ref, send_ref, sums_ref), outs, (hold, part) = refs[:3], refs[3 : 3 + nd], refs[3 + nd :]
    width, tok = za_ref.shape[1], send_ref.shape[0]
    take_rows(ins, hold)
    for at, here in lanes(width):
        dw = inverse(ins, hold, tqt_ref, here)
        za, zha = za_ref[:, here].astype(F32), zha_ref[:, here].astype(F32)
        zv, zhv = zv_ref[:, here].astype(F32), zhv_ref[:, here].astype(F32)
        ta = taps_ref[:, mine(0, width, at, here.size)]
        tv = taps_ref[:, mine(4 * width, width, at, here.size)]
        emit(dw, conv_wide(zv, zhv, tv), za, zha, ta, here, du_ref, sums_ref)
        emit(dw, conv_wide(za, zha, ta), zv, zhv, tv, pl.ds(width + at, here.size), du_ref, sums_ref)
    send_ref[...] = du_ref[part_of(1 - lax.axis_index("core"), tok), :]
    multiply(xt_ref, du_ref, outs, part)


def two_parts(value):
    high = rounded(value)
    return [high, value - high]


def tap_rows(every, width, rows):
    lines = []
    for at in range(0, every.shape[1], width):
        lines += two_parts(every[:, at : at + width])
    if rows > 3 * len(lines):
        lines.append(jnp.zeros((rows - 3 * len(lines), width), F32))
    return jnp.concatenate(lines, axis=0).astype(BF)


def taps_of(sums, out_ref):
    width = sums.shape[1]
    for run in range(out_ref.shape[1] // width):
        out_ref[:, run * width : (run + 1) * width] = sums[6 * run : 6 * run + 3] + sums[6 * run + 3 : 6 * run + 6]


def value_out_kernel(n, skip, off, *refs):
    ins, refs = refs[:n], refs[n + skip :]
    (tqt_ref, zg_ref, zhg_ref, taps_ref, og_ref, h1_ref, h2_ref), refs = refs[:7], refs[7:]
    (mo_ref, ms_ref, du_ref, send_ref, sums_ref), (hold, mixed) = refs[:5], refs[5:]
    core, tok, half = lax.axis_index("core"), mo_ref.shape[0], zg_ref.shape[1]
    width = mo_ref.shape[1]
    take_rows(ins, hold)
    for at, here in lanes(width):
        there = pl.ds(off + at, here.size)
        h4 = inverse(ins, hold, tqt_ref, here)
        z, zh = zg_ref[:, there].astype(F32), zhg_ref[:, there].astype(F32)
        cols = mine(2 * half, half, off + at, here.size)
        whole = mine(0, half, off + at, here.size)
        taps = taps_ref[:, cols]
        mixed[:, here] = (short_conv(z, zh, taps) * h4[0]).astype(BF)
        before, after = ordered(h1_ref[:, whole].astype(F32), h2_ref[:, whole].astype(F32))
        og = (og_ref[:, there].astype(F32), before[2:3], after[2:3])
        emit(h4, og, z, zh, taps, here, du_ref, sums_ref)
    mo_ref[...] = mixed[part_of(core, tok), :]
    ms_ref[...] = mixed[part_of(1 - core, tok), :]
    send_ref[...] = du_ref[part_of(1 - core, tok), :]


def w_grad_kernel(skip, known, *refs):
    refs = refs[skip:]
    (xt_ref, du_ref), known, outs, part = refs[:2], refs[2 : 2 + known], refs[2 + known : -1], refs[-1]
    multiply(xt_ref, du_ref, outs, part)
    if known:
        width = du_ref.shape[1]
        av = known[0][...]
        half = av.shape[1] // 2
        every = [av[:, :half], *(ref[...] for ref in known[1:]), av[:, half:]]
        rows = part.shape[0] // lax.axis_size("dp")
        extra = outs[0].shape[-2] - rows
        block = tap_rows(jnp.concatenate(every, axis=1), width, extra)
        for _, out in pieces(outs, "dp"):
            out[rows : rows + extra, :] = block


def in_part(du_ref, rows, w_ref, columns, width):
    total = None
    for run, start in enumerate(columns):
        w = w_ref[:, pl.ds(pl.multiple_of(start, 128), width)]
        part = dot_nt(du_ref[rows, run * width : (run + 1) * width], w)
        total = part if total is None else total + part
    return total


def in_first_kernel(du_ref, got_ref, w_ref, after_ref, acc_ref):
    core, tok, width = lax.axis_index("core"), got_ref.shape[0], w_ref.shape[1] // 6
    every = pl.ds(0, tok)
    own = in_part(du_ref, part_of(core, tok), w_ref, [core * width, (4 + core) * width], width)
    acc_ref[...] = own + in_part(got_ref, every, w_ref, [(1 - core) * width, (5 - core) * width], width)


def in_last_kernel(nw, *refs):
    dus, gots, owns, others = (refs[i * nw : (i + 1) * nw] for i in range(4))
    w_ref, acc_ref, after_ref, out_ref, mixed_ref, done_ref = refs[4 * nw :]
    core, half = lax.axis_index("core"), w_ref.shape[1] // 6
    tok, width = gots[0].shape
    total = acc_ref[...]
    for i in range(nw):
        for ref, rows, owner in (
            (dus[i], part_of(core, tok), core),
            (gots[i], pl.ds(0, tok), 1 - core),
        ):
            total = total + in_part(ref, rows, w_ref, [(2 + owner) * half + i * width], width)
        for ref, owner in ((owns[i], core), (others[i], 1 - core)):
            at = pl.multiple_of(owner * half + i * width, 128)
            mixed_ref[:, pl.ds(at, width)] = ref[...]
    out_ref[...] = total.astype(BF)
    done_ref[...] = jnp.zeros(done_ref.shape, F32)


def add_all(values):
    while len(values) > 1:
        values = [one + two for one, two in zip(values[::2], values[1::2])]
    return values[0]


def fold_kernel(na, n, nw, *refs):
    av, refs = [ref for _, ref in pieces(refs[:na], "dp")], refs[na:]
    gs = [[ref for _, ref in pieces(refs[i * n : (i + 1) * n], "dp")] for i in range(nw)]
    own_ref, send_ref, taps_ref, hold = refs[n * nw :]
    core, width = lax.axis_index("core"), gs[0][0].shape[1]
    half_cols = width * nw
    rows = av[0].shape[0]
    both = add_all([ref[...].astype(F32) for ref in av]).astype(BF)
    hold[:, 0:half_cols] = both[:, :half_cols]
    for i, parts in enumerate(gs):
        at = half_cols + i * width
        hold[:, at : at + width] = add_all([ref[0:rows, :].astype(F32) for ref in parts]).astype(BF)
    hold[:, 2 * half_cols :] = both[:, half_cols:]
    half = own_ref.shape[0]
    own_ref[...] = hold[part_of(core, half), :]
    send_ref[...] = hold[part_of(1 - core, half), :]
    extra = gs[-1][0].shape[0] - rows
    sums = add_all([ref[rows : rows + extra, :].astype(F32) for ref in gs[-1]])
    taps_of(sums, taps_ref)


def spread(own_ref, got_ref, out_ref):
    core, width = lax.axis_index("core"), own_ref.shape[1] // 3
    for run in range(3):
        cols = pl.ds(run * width, width)
        for ref, owner in ((own_ref, core), (got_ref, 1 - core)):
            at = pl.multiple_of((2 * run + owner) * width, 128)
            out_ref[:, pl.ds(at, width)] = ref[:, cols]


def join_kernel(own_ref, got_ref, taps_ref, *refs):
    outs, hold = refs[:-1], refs[-1]
    spread(own_ref, got_ref, hold)
    rows, width = hold.shape[0], outs[0].shape[1]
    block = tap_rows(taps_ref[...], width, outs[0].shape[0] - rows)
    for there, out in pieces(outs, "z"):
        out[0:rows, :] = hold[:, part_of(there, width)]
        out[rows:, :] = block


def sum_kernel(n, *refs):
    ins, (own_ref, send_ref, taps_ref) = refs[:n], refs[n + 1 :]
    core, (rows, width) = lax.axis_index("core"), own_ref.shape
    for out, owner in ((own_ref, core), (send_ref, 1 - core)):
        cols = part_of(owner, width)
        out[...] = add_all([ref[0:rows, cols].astype(F32) for ref in ins])
    taps_of(add_all([ref[rows:, :].astype(F32) for ref in ins]), taps_ref)


def last_kernel(factor, own_ref, got_ref, t_own_ref, t_got_ref, out_ref, taps_ref):
    core, rows = lax.axis_index("core"), own_ref.shape[0]
    out_ref[part_of(core, rows), :] = own_ref[...] * factor
    out_ref[part_of(1 - core, rows), :] = got_ref[...] * factor
    spread(t_own_ref, t_got_ref, taps_ref)
    taps_ref[...] = taps_ref[...] * factor


def shards(nw, inputs, out_grad, w_in, taps, filt):
    tok, width = inputs.shape[1], inputs.shape[2]
    ndp, nz, ncore = lax.axis_size("dp"), lax.axis_size("z"), lax.axis_size("core")
    nseq = nz * ncore
    span, each = filt.shape[0], filt.shape[1]
    seq = ("z", "core")
    core = lax.axis_index("core")
    factor = 1.0 / math.sqrt(ndp * nseq * tok)
    wide, count = width // ncore, tok * ncore
    blocks, rows = count // BLK, each * ncore
    group = math.gcd(rows, 16)
    tq, tp = dct_table(BLK), dct_table(span)
    kron = np.kron(tp.astype(np.float32), np.eye(group, dtype=np.float32)).astype(BF)
    tq, tqt, kron, kront = (jnp.asarray(table) for table in (tq, tq.T.copy(), kron, kron.T.copy()))
    x, og = inputs[0], out_grad[0]

    def S(shape, dtype=BF):
        return jax.ShapeDtypeStruct(shape, dtype)

    def call(kernel, name, ins, outs, flops, scratch=(), shade=1):
        moved = sum(a.size * a.dtype.itemsize for a in (*ins, *outs))
        whole = pl.BlockSpec(memory_space=pltpu.VMEM)
        return pl.pallas_call(
            kernel,
            out_shape=outs,
            in_specs=[whole] * len(ins),
            out_specs=[whole] * len(outs),
            scratch_shapes=scratch,
            compiler_params=pltpu.CompilerParams(**PARAMS),
            cost_estimate=pl.CostEstimate(flops=flops // shade, bytes_accessed=moved // shade, transcendentals=0),
            name=name,
        )(*ins)

    def flip(value):
        return lax.ppermute(value, "core", [(0, 1), (1, 0)])

    def swap(parts, axis):
        size = lax.axis_size(axis)
        if len(parts) == 1:
            return [lax.all_to_all(parts[0], axis, 0, 0, tiled=True)]
        return [parts[0]] + [
            lax.ppermute(parts[k], axis, [(i, i ^ k) for i in range(size)]) for k in range(1, size)
        ]

    def parts_of(whole, axis, shape):
        size = lax.axis_size(axis)
        return [S((size, *shape))] if whole else [S(shape)] * size

    mm = 2 * tok * width * width
    xs = flip(x)
    ends, og_send = call(pack_kernel, "pack", (x, og), [S((EDGE, width)), S((tok, wide))], mm // 999)
    odd = range(1, nseq - 1, 2)
    near = [(i, i + 1) for i in odd] + [(i + 1, i) for i in odd]
    far = [(i, i + 2) for i in odd] + [(i + 1, i - 1) for i in odd]
    h1, h2 = lax.ppermute(ends, seq, near), lax.ppermute(ends, seq, far)
    ogs = flip(og_send)

    def hold_of(cols):
        return pltpu.VMEM((blocks, BLK, cols), BF)

    act, edge = S((count, wide)), S((EDGE, wide))
    e_parts = parts_of(E_WHOLE, "z", (blocks, rows, wide))
    *he, zg, zhg, og_all = call(
        functools.partial(grad_block_kernel, len(e_parts)), "grad_block",
        (x, xs, h1, h2, w_in, taps, og, ogs, tq), e_parts + [act, edge, act],
        mm + mm // 4, [hold_of(wide)],
    )
    ce = swap(he, "z")
    some = wide // nw
    w_parts = parts_of(W_WHOLE, "z", (blocks, rows, some))
    *hw, za, zv, zha, zhv, xt = call(
        functools.partial(value_block_kernel, len(w_parts), nw), "value_block",
        (x, xs, h1, h2, w_in, taps, tq, zhg),
        w_parts * nw + [act, act, edge, edge, S((width, count))],
        2 * mm + mm // 4, [hold_of(wide)],
    )
    cw = [swap(hw[i * len(w_parts) : (i + 1) * len(w_parts)], "z") for i in range(nw)]
    filts = flip(lax.dynamic_slice_in_dim(filt, (1 - core) * wide, wide, axis=2))

    def span_step(parts, off, *after):
        cols = parts[0].shape[-1]
        return call(
            functools.partial(span_kernel, len(parts), len(after), off), "span",
            (*parts, *after, filt, filts, kron, kront, tq),
            parts_of(len(parts) == 1, "z", (blocks * rows + EDGE, cols)), mm // 2,
            [pltpu.VMEM((span, rows, cols), BF), pltpu.VMEM((span, rows, cols), BF if each % 16 == 0 else F32)],
        )

    se = span_step(ce, 0, zha)
    be = swap(se, "z")
    sw, bw, behind = [], [], se[0]
    for i in range(nw):
        sw.append(span_step(cw[i], i * some, behind))
        bw.append(swap(sw[i], "z"))
        behind = sw[i][0]

    high = width // ndp
    av_parts = parts_of(AV_WHOLE, "dp", (high, width))
    du, send, s_av, *p_av = call(
        functools.partial(grad_out_kernel, len(be), len(av_parts)), "grad_out",
        (*be, behind, tqt, za, zv, zha, zhv, taps, xt),
        [S((count, width)), S((tok, width)), S((3, width), F32)] + av_parts,
        2 * mm, [hold_of(wide), pltpu.VMEM((width, width), BF)], SHADE,
    )
    r_av = swap(p_av, "dp")
    du_av, got_av = du, flip(send)

    dus, gots, owns, others, known, r_g, behind = [], [], [], [], [s_av], [], r_av[1:AV_DONE]
    after = p_av[:1]
    for i in range(nw):
        ends_here = i == nw - 1
        extra = -(-6 * 3 * nw // 16) * 16 if ends_here else 0
        g_parts = parts_of(G_WHOLE, "dp", (high + extra, some))
        m_own, m_send, du, send, sums = call(
            functools.partial(value_out_kernel, len(bw[i]), len(after), i * some), "value_out",
            (*bw[i], *after, tqt, zg, zhg, taps, og_all, h1, h2),
            [S((tok, some))] * 2 + [S((count, some)), S((tok, some)), S((3, some), F32)],
            mm // 2, [hold_of(some), pltpu.VMEM((count, some), BF)],
        )
        known.append(sums)
        extra_in = known if ends_here else []
        p_g = call(
            functools.partial(w_grad_kernel, len(behind), len(extra_in)), "w_grad",
            (*behind, xt, du, *extra_in), g_parts, mm, [pltpu.VMEM((width, some), BF)],
        )
        r_g += swap(p_g, "dp")
        dus.append(du)
        gots.append(flip(send))
        owns.append(m_own)
        others.append(flip(m_send))
        after, behind = p_g[:1], p_g[:1]
    acc = call(in_first_kernel, "in_first", (du_av, got_av, w_in, *behind), [S((tok, width), F32)], 2 * mm)[0]
    in_grad, mixed, done = call(
        functools.partial(in_last_kernel, nw), "in_last",
        (*dus, *gots, *owns, *others, w_in, acc, *behind), [S((tok, width))] * 2 + [S((8, 128), F32)], mm,
    )

    cols, half = 3 * wide, high // ncore
    w_own, w_send, t_own = call(
        functools.partial(fold_kernel, len(r_av), len(r_g) // nw, nw), "fold", (*r_av, *r_g),
        [S((half, cols)), S((half, cols)), S((3, cols), F32)], mm // 64, [pltpu.VMEM((high, cols), BF)],
    )

    w_got = flip(w_send)
    mine_of = 3 * width // nseq
    if mine_of % 128 == 0:
        runs = cols // (ncore * mine_of)
        lines = half + -(-6 * runs // 16) * 16
        sent = call(
            join_kernel, "join", (w_own, w_got, t_own), [S((lines, ncore * mine_of))] * nz, mm // 64,
            [pltpu.VMEM((half, 3 * width), BF)],
        )
        total, send, t_own = call(
            functools.partial(sum_kernel, nz), "sum", (*swap(sent, "z"), done),
            [S((half, mine_of), F32)] * 2 + [S((3, cols), F32)], mm // 64,
        )
        w_in_grad, taps_grad = call(
            functools.partial(last_kernel, factor), "last", (total, flip(send), t_own, flip(t_own)),
            [S((high, mine_of), F32), S((3, 3 * width), F32)], mm // 64,
        )
    else:

        def joined(own, got):
            own, got = own.reshape(-1, 3, 1, wide), got.reshape(-1, 3, 1, wide)
            low, high = jnp.where(core == 0, own, got), jnp.where(core == 0, got, own)
            return jnp.concatenate([low, high], axis=2).reshape(-1, 3 * width)

        step = 1
        while step < nz:
            t_own = t_own + lax.ppermute(t_own, "z", [(i, i ^ step) for i in range(nz)])
            step *= 2
        taps_grad = joined(t_own, flip(t_own)) * factor
        sent = joined(w_own, w_got).reshape(half, nseq, mine_of).transpose(1, 0, 2)
        got = lax.all_to_all(sent, seq, 0, 0, tiled=True).reshape(nz, high, mine_of)
        w_in_grad = jnp.sum(got.astype(F32), axis=0) * factor
    return (mixed[None], in_grad[None], w_in_grad, taps_grad)


def solution(mesh):
    ndp, nseq = mesh.shape["dp"], mesh.shape["seq"]
    split = Mesh(mesh.devices.reshape(ndp, nseq // 2, 2), ("dp", "z", "core"))
    seq = ("z", "core")
    return jax.shard_map(
        functools.partial(shards, NW),
        mesh=split,
        in_specs=(P("dp", seq, None), P("dp", seq, None), P(), P(), P(None, seq, None)),
        out_specs=(P("dp", seq, None), P("dp", seq, None), P("dp", seq), P()),
        check_vma=False,
    )
```
